32 devices in a mesh: seq: 8 (over y, x, core), grp: 4 (over z).
Axes of the slice: x: 2, y: 2, z: 4, core: 2. Of those that a mesh axis runs over, the one named last changes fastest.
Arguments:
- tokens: bfloat16 [768, 32768], P('grp', 'seq'), may hold values from -6 to 6
- cotangent: bfloat16 [768, 32768], P('grp', 'seq'), may hold values from -6 to 6
- lengths: int32 [64], P('seq'), may hold values from 64 to 512, as said below
- w_query: bfloat16 [768, 192], P('grp'), may hold values from -0.4375 to 0.4375
- w_key: bfloat16 [768, 192], P('grp'), may hold values from -0.4375 to 0.4375
- w_value: bfloat16 [768, 192], P('grp'), may hold values from -0.4375 to 0.4375
- b_query: float32 [768], P('grp'), may hold values from -3 to 3
- b_value: float32 [768], P('grp'), may hold values from -3 to 3
- w_out: bfloat16 [768, 768], P('grp'), may hold values from -1.75 to 1.75
- b_out: float32 [768], P('grp'), may hold values from -3 to 3
- gain_attn: float32 [768], P('grp'), may hold values from 0.5 to 1.5
- shift_attn: float32 [768], P('grp'), may hold values from -3 to 3
- w_inter: bfloat16 [768, 768], P('grp'), may hold values from -0.4375 to 0.4375
- b_inter: float32 [3072], P('grp'), may hold values from -3 to 3
- w_back: bfloat16 [768, 768], P('grp'), may hold values from -0.21875 to 0.21875
- b_back: float32 [768], P('grp'), may hold values from -3 to 3
- gain_ffn: float32 [768], P('grp'), may hold values from 0.5 to 1.5
- shift_ffn: float32 [768], P('grp'), may hold values from -3 to 3
Outputs:
- result: bfloat16 [768, 32768], P('grp', 'seq')
- grad_tokens: float32 [768, 32768], P('grp', 'seq')
- grad_w_query: float32 [768, 192], P('grp')
- grad_w_key: float32 [768, 192], P('grp')
- grad_w_value: float32 [768, 192], P('grp')
- grad_b_query: float32 [768], P('grp')
- grad_b_value: float32 [768], P('grp')
- grad_w_out: float32 [768, 768], P('grp')
- grad_b_out: float32 [768], P('grp')
- grad_gain_attn: float32 [768], P('grp')
- grad_shift_attn: float32 [768], P('grp')
- grad_w_inter: float32 [768, 768], P('grp')
- grad_b_inter: float32 [3072], P('grp')
- grad_w_back: float32 [768, 768], P('grp')
- grad_b_back: float32 [768], P('grp')
- grad_gain_ffn: float32 [768], P('grp')
- grad_shift_ffn: float32 [768], P('grp')
The draws below stay inside these ranges and needn't reach their ends.
Inputs may be any that keep to these rules, and one draw needn't show every extreme that they name: `lengths`: slots of a sequence at or past its length are padding; some sequence has 512 tokens and some has 64.
All inputs are finite; a program needn't handle non-finite values.
Results may differ from the reference program's by a relative error of at most 0.013.
Values may be sent and summed in bfloat16 or wider, within the bound.
A program may use at most 128 MiB of HBM per device.

```python
from functools import partial
import jax
import jax.numpy as jnp
from jax import lax

D = 768
HEADS = 12
HEAD_DIM = 64
FF = 3072
GROUPS = 4
LEN = 512
SEQS = 64
TOKENS = 32768
CG = 192
FG = 768


def draw_lengths(key, part):
    key = jax.random.fold_in(key, 7)
    first_key, second_key, third_key = jax.random.split(key, 3)
    drawn = jax.random.randint(first_key, (SEQS,), LEN // 8, LEN + 1)
    longest = jax.random.randint(second_key, (), 0, SEQS)
    offset = jax.random.randint(third_key, (), 1, SEQS)
    shortest = (longest + offset) % SEQS
    places = jnp.arange(SEQS)
    drawn = jnp.where(places == longest, LEN, drawn)
    drawn = jnp.where(places == shortest, LEN // 8, drawn)
    return drawn.astype(jnp.int32)


def block_scale(stream_key, extent, shards, low, high):
    level, own = 1.0, jax.random.fold_in(stream_key, 6)
    for dim, blocks in shards:
        heights = jnp.exp(jax.random.uniform(jax.random.fold_in(own, dim), (blocks,), jnp.float32, low / len(shards), high / len(shards)))
        level = level * jnp.repeat(heights, extent[dim] // blocks).reshape([-1 if axis == dim else 1 for axis in range(len(extent))])
    return level


def scatter_about(own_key, shape, scale, most, cuts=(), kind=jnp.bfloat16):
    level = block_scale(own_key, shape, cuts, -0.22, 0.18) if cuts else 1.0
    values = jax.random.normal(own_key, shape, jnp.float32) * scale * level
    return jnp.minimum(jnp.maximum(values, -most), most).astype(kind)


def setup_inputs(seed: int = 0) -> dict:
    key_of = jax.random.split(jax.random.key(seed), 19)
    return {
        "tokens": scatter_about(key_of[0], (D, TOKENS), 1.0, 6.0, ((0, 4), (1, 8))),
        "cotangent": scatter_about(key_of[1], (D, TOKENS), 1.0, 6.0, ((0, 4), (1, 8))),
        "lengths": draw_lengths(jax.random.fold_in(key_of[18], 71), 0),
        "w_query": scatter_about(key_of[3], (D, CG), CG ** -0.5, 0.4375, ((0, 4),)),
        "w_key": scatter_about(key_of[4], (D, CG), CG ** -0.5, 0.4375, ((0, 4),)),
        "w_value": scatter_about(key_of[5], (D, CG), CG ** -0.5, 0.4375, ((0, 4),)),
        "b_query": scatter_about(key_of[6], (D,), 0.3, 3.0, ((0, 4),), jnp.float32),
        "b_value": scatter_about(key_of[7], (D,), 0.3, 3.0, ((0, 4),), jnp.float32),
        "w_out": scatter_about(key_of[8], (D, D), (D * 8 // LEN) ** -0.5, 1.75, ((0, 4),)),
        "b_out": scatter_about(key_of[9], (D,), 0.3, 3.0, ((0, 4),), jnp.float32),
        "gain_attn": jnp.clip(1.0 + 0.1 * jax.random.normal(key_of[10], (D,), jnp.float32), 0.5, 1.5),
        "shift_attn": scatter_about(key_of[11], (D,), 0.3, 3.0, ((0, 4),), jnp.float32),
        "w_inter": scatter_about(key_of[12], (D, FG), CG ** -0.5, 0.4375, ((0, 4),)),
        "b_inter": scatter_about(key_of[13], (FF,), 0.3, 3.0, ((0, 4),), jnp.float32),
        "w_back": scatter_about(key_of[14], (D, FG), FG ** -0.5, 0.21875, ((0, 4),)),
        "b_back": scatter_about(key_of[15], (D,), 0.3, 3.0, ((0, 4),), jnp.float32),
        "gain_ffn": jnp.clip(1.0 + 0.1 * jax.random.normal(key_of[16], (D,), jnp.float32), 0.5, 1.5),
        "shift_ffn": scatter_about(key_of[17], (D,), 0.3, 3.0, ((0, 4),), jnp.float32),
    }


@jax.custom_vjp
def low(v):
    return lax.optimization_barrier(v.astype(jnp.bfloat16)).astype(jnp.float32)

@jax.custom_vjp
def low_back(v):
    return v

def low_keep(v):
    return (low(v), None)

def low_pass(kept, grad):
    return (grad,)

def back_keep(v):
    return (v, None)

def back_low(kept, grad):
    return (low(grad),)
low.defvjp(low_keep, low_pass)
low_back.defvjp(back_keep, back_low)
highest = lax.Precision.HIGHEST
eps_norm = 1e-12

def group_conv(inputs, kernel, width_in, width_out):
    rows = inputs.shape[0]
    pieces = inputs.reshape(rows, GROUPS, width_in)
    return jnp.einsum('tgc,gcd->tgd', pieces, kernel, precision=highest).reshape(rows, GROUPS * width_out)

def layer_norm(resid, gain, shift):
    center = resid - lax.optimization_barrier(jnp.mean(resid, axis=1, keepdims=True))
    spread = lax.optimization_barrier(jnp.mean(center * center, axis=1, keepdims=True))
    return center * lax.rsqrt(spread + eps_norm) * gain + shift

def attend_block(packed):
    queries, key_rows, val_rows, seq_lengths = packed
    raw = jnp.einsum('bqhe,bkhe->bhqk', queries, key_rows, precision=highest)
    scores = low_back(raw) * HEAD_DIM ** (-0.5)
    places = jnp.arange(LEN, dtype=jnp.int32)
    valid = places[None, :] < seq_lengths[:, None]
    scores = jnp.where(valid[:, None, None, :], scores, -1e+30)
    top = lax.optimization_barrier(jnp.max(scores, axis=-1, keepdims=True))
    expo = jnp.exp(scores - top)
    probs = expo / lax.optimization_barrier(jnp.sum(expo, axis=-1, keepdims=True))
    return jnp.einsum('bhqk,bkhe->bqhe', low(probs), val_rows, precision=highest)

def layer(lengths, tokens_cols, w_query, w_key, w_value, b_query, b_value, w_out, b_out, gain_attn, shift_attn, w_inter, b_inter, w_back, b_back, gain_ffn, shift_ffn):
    group_width = D // GROUPS
    hidden_width = FF // GROUPS
    tokens = tokens_cols.T
    kernel_q = w_query.reshape(GROUPS, group_width, group_width)
    kernel_k = w_key.reshape(GROUPS, group_width, group_width)
    kernel_v = w_value.reshape(GROUPS, group_width, group_width)
    kernel_i = w_inter.reshape(GROUPS, group_width, hidden_width)
    kernel_b = jnp.transpose(w_back.reshape(GROUPS, group_width, hidden_width), (0, 2, 1))
    queries = low_back(low(group_conv(tokens, kernel_q, group_width, group_width) + b_query))
    key_rows = low_back(low(group_conv(tokens, kernel_k, group_width, group_width)))
    val_rows = low_back(low(group_conv(tokens, kernel_v, group_width, group_width) + b_value))
    batch = 8
    shaped = (SEQS // batch, batch, LEN, HEADS, HEAD_DIM)
    context = lax.map(jax.checkpoint(attend_block), (queries.reshape(shaped), key_rows.reshape(shaped), val_rows.reshape(shaped), lengths.reshape(SEQS // batch, batch)))
    context = low_back(low(context.reshape(TOKENS, D)))
    branch = low_back(jnp.dot(context, w_out.T, precision=highest) + b_out)
    middle = layer_norm(tokens + branch, gain_attn, shift_attn)
    inner = low_back(group_conv(low(middle), kernel_i, group_width, hidden_width) + b_inter)
    active = low(jax.nn.gelu(inner, approximate=False))
    ffn_out = low_back(group_conv(active, kernel_b, hidden_width, group_width) + b_back)
    return layer_norm(middle + ffn_out, gain_ffn, shift_ffn).T

def reference(tokens, cotangent, lengths, w_query, w_key, w_value, b_query, b_value, w_out, b_out, gain_attn, shift_attn, w_inter, b_inter, w_back, b_back, gain_ffn, shift_ffn):
    floats = [arr.astype(jnp.float32) for arr in (tokens, w_query, w_key, w_value, b_query, b_value, w_out, b_out, gain_attn, shift_attn, w_inter, b_inter, w_back, b_back, gain_ffn, shift_ffn)]
    result, pull = jax.vjp(partial(layer, lengths), *floats)
    grads = pull(cotangent.astype(jnp.float32))
    grad_tokens, grad_w_query, grad_w_key, grad_w_value, grad_b_query, grad_b_value, grad_w_out, grad_b_out, grad_gain_attn, grad_shift_attn, grad_w_inter, grad_b_inter, grad_w_back, grad_b_back, grad_gain_ffn, grad_shift_ffn = grads
    return (result.astype(jnp.bfloat16), grad_tokens, grad_w_query, grad_w_key, grad_w_value, grad_b_query, grad_b_value, grad_w_out, grad_b_out, grad_gain_attn, grad_shift_attn, grad_w_inter, grad_b_inter, grad_w_back, grad_b_back, grad_gain_ffn, grad_shift_ffn)
```

```python
import functools
import math

import jax
import jax.numpy as jnp
from jax import lax
from jax.experimental import pallas as pl
from jax.experimental.pallas import tpu as pltpu
from jax.sharding import PartitionSpec as P

HEAD_DIM = 64
EPS = 1e-12
MASKED = -1e30
F32, LOW = jnp.float32, jnp.bfloat16
VMEM_BYTES = 60 * 1024 * 1024
MESH = pl.DeviceIdType.MESH
BLOCK = 256
ERF_P = 0.3275911
ERF_A = (0.254829592, -0.284496736, 1.421413741, -1.453152027, 1.061405429)
B_QUERY, B_VALUE, B_OUT, GAIN1, SHIFT1, B_BACK, GAIN2, SHIFT2, B_INTER = range(9)
VECTORS, VECTOR_COUNT = 16, 9


def mm(left, right):
    return jnp.dot(left, right, preferred_element_type=F32)


def mm_tn(left, right):
    return lax.dot_general(left, right, (((0,), (0,)), ((), ())), preferred_element_type=F32)


def mm_nt(left, right):
    return lax.dot_general(left, right, (((1,), (1,)), ((), ())), preferred_element_type=F32)


def round_up(value, unit):
    return -(-value // unit) * unit


def bit(value, unit):
    if isinstance(value, int):
        return value // unit % 2
    return lax.rem(lax.div(value, jnp.int32(unit)), jnp.int32(2))


def xor(left, right, size):
    total, unit = 0, 1
    while unit < size:
        total = total + unit * ((bit(left, unit) + bit(right, unit)) % 2)
        unit *= 2
    return total


class Plane:
    def __init__(self, size, rows):
        self.size, self.pairs = size, size // 2
        self.row_parts = min(4, self.pairs)
        self.col_parts = self.pairs // self.row_parts
        self.rows = rows // self.row_parts

    def padded(self, columns):
        return 2 * round_up(round_up(columns, 256) // 2, 128 * self.col_parts)

    def piece(self, index, columns):
        width = columns // self.col_parts
        down, along = lax.rem(index, self.row_parts), lax.div(index, self.row_parts)
        if self.col_parts == 1:
            along = 0
        return down * self.rows, along * width, width


def ds(start, size, unit):
    return pl.ds(start if isinstance(start, int) else pl.multiple_of(start, unit), size)


def remote(src, dst, send, recv, device):
    return pltpu.make_async_remote_copy(
        src_ref=src, dst_ref=dst, send_sem=send, recv_sem=recv, device_id=device, device_id_type=MESH
    )


def in_turn(me, start):
    middle = (me == 1) | (me == 2)

    @pl.when(middle)
    def _():
        for j in (2, 1, 3):
            start(j)

    @pl.when(jnp.logical_not(middle))
    def _():
        for j in (1, 2, 3):
            start(j)


def greet(devices):
    barrier = pltpu.get_barrier_semaphore()
    for device in devices:
        pl.semaphore_signal(barrier, inc=1, device_id=device, device_id_type=MESH)


def meet(devices):
    pl.semaphore_wait(pltpu.get_barrier_semaphore(), len(devices))


def in_plane(side, pairs, start):
    first = [k for k in (1, 2) if k < pairs]
    rest = range(3, pairs)

    @pl.when(side == 0)
    def _():
        for k in (*first, *rest):
            start(k)

    @pl.when(side == 1)
    def _():
        for k in (*first[::-1], *rest):
            start(k)


def gelu_parts(inner):
    below = 1.0 + (ERF_P / math.sqrt(2.0)) * jnp.abs(inner)
    t = pl.reciprocal(below, approx=True)
    t = t * (2.0 - below * t)
    bell = jnp.exp(-0.5 * inner * inner)
    poly = 0.5 * ERF_A[4]
    for coeff in ERF_A[3::-1]:
        poly = poly * t + 0.5 * coeff
    tail = poly * t * bell
    below = jnp.where(inner < 0, tail, 1.0 - tail)
    return inner * below, below + inner * bell * (1.0 / math.sqrt(2.0 * math.pi))


def forward_kernel(
    groups,
    plane,
    seq_len,
    len_ref,
    tok_ref,
    cot_ref,
    w_out_ref,
    w_inter_ref,
    w_back_ref,
    w_query_ref,
    w_key_ref,
    w_value_ref,
    *refs,
):
    vector_refs, refs = refs[0:VECTOR_COUNT], refs[VECTOR_COUNT:]
    forward_body(
        groups,
        plane,
        seq_len,
        len_ref,
        tok_ref,
        cot_ref,
        (w_out_ref, w_inter_ref, w_back_ref),
        (w_query_ref, w_key_ref, w_value_ref),
        vector_refs,
        *refs,
    )


def forward_body(
    groups,
    plane,
    seq_len,
    len_ref,
    tok_ref,
    cot_ref,
    rest_refs,
    qkv_any,
    vector_any,
    cots_out,
    toks_out,
    wq_out,
    inter_out,
    back_t_out,
    out_t_out,
    vecs_out,
    placed_out,
    result_out,
    mid_low_out,
    normed1_out,
    normed2_out,
    active_out,
    slope_out,
    qkv_ref,
    expo_ref,
    inv_ref,
    ctx_ref,
    invs_ref,
    result_ref,
    mid_low_ref,
    normed1_ref,
    normed2_ref,
    active_ref,
    slope_ref,
    save_sem,
    toks,
    wq,
    rest,
    vec_rows,
    vecs,
    placed,
    inter_t,
    back_t,
    out_t,
    resid,
    qkv_refs,
    *rest_of_scratch,
):
    vector_refs = rest_of_scratch[0:VECTOR_COUNT]
    forward_steps(
        groups,
        plane,
        seq_len,
        len_ref,
        tok_ref,
        cot_ref,
        rest_refs,
        qkv_any,
        vector_any,
        (cots_out, toks_out, wq_out, inter_out, back_t_out, out_t_out, vecs_out, placed_out),
        (result_out, mid_low_out, normed1_out, normed2_out, active_out, slope_out),
        (qkv_ref, expo_ref, inv_ref, ctx_ref, invs_ref),
        (result_ref, mid_low_ref, normed1_ref, normed2_ref, active_ref, slope_ref, save_sem),
        (toks, wq, rest, vec_rows, vecs, placed, inter_t, back_t, out_t, resid),
        qkv_refs,
        vector_refs,
        *rest_of_scratch[VECTOR_COUNT:],
    )


def forward_steps(
    groups,
    plane,
    seq_len,
    len_ref,
    tok_ref,
    cot_ref,
    rest_refs,
    qkv_any,
    vector_any,
    outs,
    saved_outs,
    blocked_outs,
    saved,
    scratch,
    qkv_refs,
    vector_refs,
    local_sem,
    tok_send,
    tok_recv,
    cot_send,
    cot_recv,
    vec_send,
    vec_recv,
    q1_send,
    q1_recv,
    q2_send,
    q2_recv,
    q3_send,
    q3_recv,
    r1_send,
    r1_recv,
    r2_send,
    r2_recv,
    r3_send,
    r3_recv,
    fused=False,
):
    cots_out, toks_out, wq_out, inter_out, back_t_out, out_t_out, vecs_out, placed_out = outs
    result_out, mid_low_out, normed1_out, normed2_out, active_out, slope_out = saved_outs
    qkv_ref, expo_ref, inv_ref, ctx_ref, invs_ref = blocked_outs
    result_ref, mid_low_ref, normed1_ref, normed2_ref, active_ref, slope_ref, save_sem = saved
    toks, wq, rest, vec_rows, vecs, placed, inter_t, back_t, out_t, resid = scratch
    width, span = toks.shape[1:]
    seqs = span // seq_len
    wide = groups * width
    hidden = active_ref.shape[1]
    heads = width // HEAD_DIM
    first_mid = groups * seqs
    last = first_mid + span // BLOCK - 1
    step = pl.program_id(0)
    me, at_plane = lax.axis_index("grp"), lax.axis_index("seq")
    side, pair = lax.rem(at_plane, 2), lax.div(at_plane, 2)
    group_device = [{"grp": xor(me, j, groups)} for j in range(groups)]
    pair_device = [{"seq": xor(at_plane, 2 * k, plane.size)} for k in range(plane.pairs)]
    partner = {"seq": xor(at_plane, 1, plane.size)}
    others = range(1, groups)

    def token_copy(j, s):
        owner = xor(me, j, groups)
        return remote(
            tok_ref.at[:, ds(owner * span + s * seq_len, seq_len, seq_len)],
            toks.at[j, :, ds(s * seq_len, seq_len, seq_len)],
            tok_send.at[j, s],
            tok_recv.at[j, s],
            group_device[j],
        )

    def cot_copy(j, s):
        start = xor(me, j, groups) * span + s * seq_len
        return remote(
            cot_ref.at[:, ds(start, seq_len, seq_len)],
            cots_out.at[j, :, ds(s * seq_len, seq_len, seq_len)],
            cot_send.at[j, s],
            cot_recv.at[j, s],
            group_device[j],
        )

    def vec_copy(j):
        source = vec_rows.at[2 if j == 3 else 0]
        device = group_device[1 if j == 3 else j]
        return remote(source, vec_rows.at[j], vec_send.at[j], vec_recv.at[j], device)

    q_rows = wq.shape[1] // plane.size

    def q_own(index, s):
        return ds((s * plane.pairs + index) * q_rows, q_rows, 16)

    def q1_copy(j):
        own = q_own(pair, side)
        source = wq.at[2 if j == 3 else 0, own, :]
        device = group_device[1 if j == 3 else j]
        return remote(source, wq.at[j, own, :], q1_send.at[j], q1_recv.at[j], device)

    q_groups = (pl.ds(1, 2), pl.ds(3, 1))

    def q2_copy(late, k, index):
        part = wq.at[q_groups[late], q_own(index, side), :]
        return remote(part, part, q2_send.at[late, k], q2_recv.at[late, k], pair_device[k])

    def q3_copy(late, s):
        rows = ds(s * plane.pairs * q_rows, plane.pairs * q_rows, 16)
        part = wq.at[q_groups[late], rows, :]
        return remote(part, part, q3_send.at[late], q3_recv.at[late], partner)

    half = rest.shape[2] // 2

    def rest_piece(index):
        down, along, size = plane.piece(index, half)
        return ds(down, plane.rows, 16), ds(side * half + along, size, 128)

    def r1_copy(j):
        down, along = rest_piece(pair)
        return remote(
            rest.at[2 if j == 3 else 0, down, along],
            rest.at[j, down, along],
            r1_send.at[j],
            r1_recv.at[j],
            group_device[1 if j == 3 else j],
        )

    def r2_copy(k, index):
        down, along = rest_piece(index)
        part = rest.at[pl.ds(1, groups - 1), down, along]
        return remote(part, part, r2_send.at[k], r2_recv.at[k], pair_device[k])

    def r3_copy(s):
        part = rest.at[pl.ds(1, groups - 1), :, ds(s * half, half, 128)]
        return remote(part, part, r3_send.at[0], r3_recv.at[0], partner)

    mine = ds(me * span, span, span)
    columns = [(0, wide), (wide, hidden), (wide + hidden, hidden)]
    local_copies = [
        (tok_ref.at[:, mine], toks.at[0]),
    ]
    local_copies += [
        (ref, rest.at[0, :, pl.ds(*place)]) for ref, place in zip(rest_refs, columns)
    ]
    local_copies += [
        (toks, toks_out),
        (wq.at[:, pl.ds(0, 3 * width), :], wq_out),
        (rest.at[:, :, pl.ds(wide, hidden)], inter_out),
        (vecs, vecs_out),
        (back_t, back_t_out),
        (out_t, out_t_out),
        (placed, placed_out),
    ]
    small = [(qkv_any[i], qkv_refs.at[i]) for i in range(3)]
    small += list(zip(vector_any, vector_refs))
    local_copies += small
    saves = [
        (result_ref, result_out),
        (mid_low_ref, mid_low_out),
        (normed1_ref, normed1_out),
        (normed2_ref, normed2_out),
        (active_ref, active_out),
        (slope_ref, slope_out),
    ]

    def save(i, b):
        part = pl.ds(b * BLOCK, BLOCK)
        source, target = saves[i]
        return pltpu.make_async_copy(
            source.at[:, :, part], target.at[:, :, part], save_sem.at[i, b]
        )

    def local_copy(i):
        return pltpu.make_async_copy(*local_copies[i], local_sem.at[i])

    @pl.when(step == 0)
    def _():
        greet(group_device[1:] + pair_device[1:] + [partner])
        smalls = range(len(local_copies) - len(small), len(local_copies))
        for i in (*smalls, 0, 1, 2, 3):
            local_copy(i).start()
        meet(group_device[1:] + pair_device[1:] + [partner])
        middle = (me == 1) | (me == 2)
        pl.when(middle)(lambda: token_copy(2, 0).start())
        pl.when(jnp.logical_not(middle))(lambda: token_copy(1, 0).start())
        vecs[...] = jnp.zeros_like(vecs)
        vec_rows[0] = jnp.zeros_like(vec_rows[0])
        for i in smalls:
            local_copy(i).wait()
        for i in range(VECTOR_COUNT - 1):
            vec_rows[0, i : i + 1, 0:width] = vector_refs[i][...]
        b_inter = jnp.concatenate([vector_refs[-1][i : i + 1] for i in range(hidden // 128)], axis=1)
        for a in range(hidden // width):
            i = B_INTER + a
            vec_rows[0, i : i + 1, 0:width] = b_inter[:, a * width : (a + 1) * width]
        for i in range(3):
            wq[0, i * width : (i + 1) * width, :] = qkv_refs[i].T
        if wq.shape[1] > 3 * width:
            wq[0, 3 * width :, :] = jnp.zeros_like(wq[0, 3 * width :, :])

        def start_small(j):
            q1_copy(j).start()
            vec_copy(j).start()

        @pl.when(middle)
        def _():
            start_small(1)
            start_small(2)

        @pl.when(jnp.logical_not(middle))
        def _():
            start_small(2)
            start_small(1)

        for i in (1, 2, 3):
            local_copy(i).wait()

        @pl.when(middle)
        def _():
            r1_copy(1).start()
            r1_copy(2).start()
            for j, s in ((2, 1), (1, 0), (1, 1)):
                token_copy(j, s).start()

        @pl.when(jnp.logical_not(middle))
        def _():
            r1_copy(2).start()
            r1_copy(1).start()
            for j, s in ((1, 1), (2, 0), (2, 1)):
                token_copy(j, s).start()

        local_copy(0).wait()
        vecs[0, :, 0:VECTORS] = vec_rows[0, :, 0:width].T

    @pl.when(step == 1)
    def _():
        for j in (1, 2):
            q1_copy(j).wait_recv()
            vec_copy(j).wait_recv()
        in_plane(side, plane.pairs, lambda k: q2_copy(0, k, pair).start())
        q1_copy(3).start()
        vec_copy(3).start()
        for j in (1, 2):
            vecs[j, :, 0:VECTORS] = vec_rows[j, :, 0:width].T

    @pl.when(step == seqs)
    def _():
        for k in range(1, plane.pairs):
            q2_copy(0, k, xor(pair, k, plane.pairs)).wait_recv()
        q3_copy(0, side).start()
        r1_copy(2).wait_recv()
        middle = (me == 1) | (me == 2)
        pl.when(jnp.logical_not(middle))(lambda: token_copy(3, 0).start())
        r1_copy(3).start()
        pl.when(middle)(lambda: token_copy(3, 0).start())
        for s in range(1, seqs):
            token_copy(3, s).start()
        q3_copy(0, 1 - side).wait_recv()

    for j in others:
        for s in range(seqs):

            @pl.when(step == j * seqs + s)
            def _():
                token_copy(j, s).wait_recv()

    @pl.when(step == 2 * seqs + 1)
    def _():
        for s in range(seqs):
            cot_copy(1, s).start()
        for s in range(seqs):
            for j in (2, 3):
                cot_copy(j, s).start()
        q1_copy(3).wait_recv()
        vec_copy(3).wait_recv()
        vecs[3, :, 0:VECTORS] = vec_rows[3, :, 0:width].T
        in_plane(side, plane.pairs, lambda k: q2_copy(1, k, pair).start())
        r1_copy(1).wait_recv()
        r1_copy(3).wait_recv()
        in_plane(side, plane.pairs, lambda k: r2_copy(k, pair).start())

    @pl.when(step == 3 * seqs)
    def _():
        for k in range(1, plane.pairs):
            q2_copy(1, k, xor(pair, k, plane.pairs)).wait_recv()
        q3_copy(1, side).start()
        q3_copy(1, 1 - side).wait_recv()

    @pl.when(step == 3 * seqs + 1)
    def _():
        for k in range(1, plane.pairs):
            r2_copy(k, xor(pair, k, plane.pairs)).wait_recv()
        r3_copy(side).start()

    @pl.when(step == first_mid)
    def _():
        r3_copy(1 - side).wait_recv()
        for i in () if fused else (4, 5, 6, 7, 10):
            local_copy(i).start()
        for g in range(groups):
            inter_t[g] = rest[g, :, wide : wide + hidden].T

    @pl.when(step == first_mid + 1)
    def _():
        for g in range(groups):
            back_t[g] = rest[g, :, wide + hidden : wide + 2 * hidden].T
            out_t[:, g * width : (g + 1) * width] = rest[g, :, 0:wide].T
        for i in () if fused else (8, 9):
            local_copy(i).start()

    @pl.when(step < first_mid)
    def _():
        j, s = lax.div(step, seqs), lax.rem(step, seqs)
        at = ds(s * seq_len, seq_len, seq_len)
        length = len_ref[me * seqs + s]
        drawn = mm(wq[j, 0 : 3 * width, :], toks[j, :, at])
        vec = vecs[j]
        qkv_ref[0, 0:width, :] = (
            (drawn[0:width] + vec[:, B_QUERY : B_QUERY + 1]) * (1.0 / math.sqrt(HEAD_DIM))
        ).astype(LOW)
        qkv_ref[0, width : 2 * width, :] = drawn[width : 2 * width].astype(LOW)
        qkv_ref[0, 2 * width :, :] = (
            drawn[2 * width :] + vec[:, B_VALUE : B_VALUE + 1]
        ).astype(LOW)
        row = lax.broadcasted_iota(jnp.int32, (16, seq_len), 0)
        place = lax.broadcasted_iota(jnp.int32, (16, seq_len), 1)
        mask_rows = jnp.where((row == 0) & (place >= length), MASKED, 0.0).astype(LOW)
        one_rows = jnp.where(row == 0, 1.0, 0.0).astype(LOW)
        inv_ref[...] = jnp.zeros_like(inv_ref)
        chunks = [(h, c) for h in range(heads) for c in range(0, seq_len, BLOCK)]

        def head(h):
            low, top = h * HEAD_DIM, (h + 1) * HEAD_DIM
            queries = jnp.concatenate([qkv_ref[0, low:top, :], one_rows], axis=0)
            keys = jnp.concatenate([qkv_ref[0, width + low : width + top, :], mask_rows], axis=0)
            values = jnp.concatenate(
                [qkv_ref[0, 2 * width + low : 2 * width + top, :], one_rows], axis=0
            )
            return queries, keys.T, values

        made = [head(0)]

        def scores_of(h, c):
            if h == len(made):
                made.append(head(h))
            queries, keys, _ = made[h]
            return mm(keys, queries[:, c : c + BLOCK])

        ready = scores_of(*chunks[0])
        for i, (h, c) in enumerate(chunks):
            scores = ready
            if i + 1 < len(chunks):
                ready = scores_of(*chunks[i + 1])
            low, top = h * HEAD_DIM, (h + 1) * HEAD_DIM
            best = jnp.max(scores, axis=0, keepdims=True)
            expo = jnp.exp(scores - best).astype(LOW)
            expo_ref[0, h, :, c : c + BLOCK] = expo
            context = mm(made[h][2], expo)
            inv = 1.0 / context[HEAD_DIM : HEAD_DIM + 1]
            inv_ref[0, h : h + 1, c : c + BLOCK] = inv
            ctx_ref[0, low:top, c : c + BLOCK] = (context[0:HEAD_DIM] * inv).astype(LOW)
        placed[ds(xor(me, j, groups) * width, width, width), at] = ctx_ref[0]

    @pl.when((step >= first_mid) & (step <= last))
    def _():
        at = ds((step - first_mid) * BLOCK, BLOCK, BLOCK)

        def column(group, which):
            return vecs[group, :, which : which + 1]

        context = placed[:, at]
        total = jnp.zeros((1, BLOCK), F32)
        for j in range(groups):
            rows = toks[j, :, at].astype(F32) + (
                mm(rest[j, :, 0:wide], context) + column(j, B_OUT)
            )
            total += jnp.sum(rows, axis=0, keepdims=True)
            resid[j] = rows
        mean = total * (1.0 / wide)
        total = jnp.zeros((1, BLOCK), F32)
        for j in range(groups):
            rows = resid[j] - mean
            total += jnp.sum(rows * rows, axis=0, keepdims=True)
        inv1 = lax.rsqrt(total * (1.0 / wide) + EPS)
        for j in range(groups):
            normed = (resid[j] - mean) * inv1
            normed1_ref[j, :, at] = normed.astype(LOW)
            rows = normed * column(j, GAIN1) + column(j, SHIFT1)
            resid[j] = rows
            mid_low_ref[j, :, at] = rows.astype(LOW)
        total = jnp.zeros((1, BLOCK), F32)
        for j in range(groups):
            for a in range(0, hidden, width):
                inner = mm(inter_t[j, a : a + width, :], mid_low_ref[j, :, at]) + column(
                    j, B_INTER + a // width
                )
                active, slope = gelu_parts(inner)
                active_ref[j, a : a + width, at] = active.astype(LOW)
                slope_ref[j, a : a + width, at] = slope.astype(LOW)
            rows = resid[j] + (
                mm(rest[j, :, wide + hidden : wide + 2 * hidden], active_ref[j, :, at])
                + column(j, B_BACK)
            )
            total += jnp.sum(rows, axis=0, keepdims=True)
            resid[j] = rows
        mean = total * (1.0 / wide)
        total = jnp.zeros((1, BLOCK), F32)
        for j in range(groups):
            rows = resid[j] - mean
            total += jnp.sum(rows * rows, axis=0, keepdims=True)
        inv2 = lax.rsqrt(total * (1.0 / wide) + EPS)
        for j in range(groups):
            normed = (resid[j] - mean) * inv2
            normed2_ref[j, :, at] = normed.astype(LOW)
            result_ref[j, :, at] = (normed * column(j, GAIN2) + column(j, SHIFT2)).astype(LOW)
        invs_ref[...] = jnp.zeros_like(invs_ref)
        invs_ref[0:1, :] = inv1
        invs_ref[1:2, :] = inv2

    for b in range(span // BLOCK):

        @pl.when(step == first_mid + b)
        def _():
            for i in range(1 if fused else len(saves)):
                save(i, b).start()

    def all_sent():
        for j in others:
            q1_copy(j).wait_send()
            vec_copy(j).wait_send()
            r1_copy(j).wait_send()
            for s in range(seqs):
                token_copy(j, s).wait_send()
                cot_copy(j, s).wait_send()
        for k in range(1, plane.pairs):
            for late in (0, 1):
                q2_copy(late, k, pair).wait_send()
            r2_copy(k, pair).wait_send()
        for late in (0, 1):
            q3_copy(late, side).wait_send()
        r3_copy(side).wait_send()

    def cots_here(s):
        for j in others:
            cot_copy(j, s).wait_recv()

    def all_saved():
        for i in range(1 if fused else len(saves)):
            for b in range(span // BLOCK):
                save(i, b).wait()

    if fused:
        return cots_here, all_saved, all_sent

    @pl.when(step == last)
    def _():
        all_sent()
        for s in range(seqs):
            cots_here(s)
        all_saved()
        for i in (4, 5, 6, 7, 8, 9, 10):
            local_copy(i).wait()


def forward(sizes, lengths, tokens, cotangent, weights, vectors):
    groups, plane, seq_len, hidden = sizes
    width, total = tokens.shape
    span = total // groups
    seqs, heads, wide = span // seq_len, width // HEAD_DIM, groups * width
    attention = groups * seqs
    steps = attention + span // BLOCK
    anywhere = pl.BlockSpec(memory_space=pl.ANY)
    wq_rows = round_up(3 * width, 16 * plane.size)
    rest_columns = plane.padded(wide + 2 * hidden)

    def group_at(t):
        return lax.div(jnp.minimum(t, attention - 1), seqs)

    def seq_at(t):
        return lax.rem(jnp.minimum(t, attention - 1), seqs)

    def block_at(t):
        return jnp.maximum(t - attention, 0)

    def by_seq(rows):
        return pl.BlockSpec((1, rows, seq_len), lambda t: (group_at(t), 0, seq_at(t)))

    def low(*shape):
        return jax.ShapeDtypeStruct(shape, LOW)

    dma = pltpu.SemaphoreType.DMA
    gate = [dma((groups,)), dma((groups,))]
    gather = gate + [dma((plane.pairs,)), dma((plane.pairs,)), dma((1,)), dma((1,))]
    gather_q = gate + [dma((2, plane.pairs)), dma((2, plane.pairs)), dma((2,)), dma((2,))]
    return pl.pallas_call(
        functools.partial(forward_kernel, groups, plane, seq_len),
        grid=(steps,),
        in_specs=[pl.BlockSpec(memory_space=pltpu.SMEM)]
        + [anywhere] * (8 + VECTOR_COUNT),
        out_specs=[anywhere] * 14
        + [
            by_seq(3 * width),
            pl.BlockSpec(
                (1, heads, seq_len, seq_len),
                lambda t: (jnp.minimum(t, attention - 1), 0, 0, 0),
            ),
            by_seq(8),
            by_seq(width),
            pl.BlockSpec((8, BLOCK), lambda t: (0, block_at(t))),
        ],
        out_shape=[
            low(groups, width, span),
            low(groups, width, span),
            low(groups, 3 * width, width),
            low(groups, width, hidden),
            low(groups, hidden, width),
            low(wide, wide),
            jax.ShapeDtypeStruct((groups, width, 128), F32),
            low(wide, span),
            low(groups, width, span),
            low(groups, width, span),
            low(groups, width, span),
            low(groups, width, span),
            low(groups, hidden, span),
            low(groups, hidden, span),
            low(groups, 3 * width, span),
            low(attention, heads, seq_len, seq_len),
            jax.ShapeDtypeStruct((groups, 8, span), F32),
            low(groups, width, span),
            jax.ShapeDtypeStruct((8, span), F32),
        ],
        scratch_shapes=[
            pltpu.VMEM((groups, width, span), LOW),
            pltpu.VMEM((groups, width, span), LOW),
            pltpu.VMEM((groups, width, span), LOW),
            pltpu.VMEM((groups, width, span), LOW),
            pltpu.VMEM((groups, hidden, span), LOW),
            pltpu.VMEM((groups, hidden, span), LOW),
            dma((6, span // BLOCK)),
            pltpu.VMEM((groups, width, span), LOW),
            pltpu.VMEM((groups, wq_rows, width), LOW),
            pltpu.VMEM((groups, width, rest_columns), LOW),
            pltpu.VMEM((groups, VECTORS, round_up(width, 128)), F32),
            pltpu.VMEM((groups, width, 128), F32),
            pltpu.VMEM((wide, span), LOW),
            pltpu.VMEM((groups, hidden, width), LOW),
            pltpu.VMEM((groups, hidden, width), LOW),
            pltpu.VMEM((wide, wide), LOW),
            pltpu.VMEM((groups, width, BLOCK), F32),
            pltpu.VMEM((3, width, width), LOW),
        ]
        + [pltpu.VMEM(vector.shape, F32) for vector in vectors]
        + [
            dma((14 + VECTOR_COUNT,)),
            dma((groups, seqs)),
            dma((groups, seqs)),
        ]
        + [dma((groups, seqs)), dma((groups, seqs))]
        + gate
        + gather_q
        + gather,
        compiler_params=pltpu.CompilerParams(
            vmem_limit_bytes=VMEM_BYTES, collective_id=0, has_side_effects=True
        ),
        name="forward",
    )(lengths, tokens, cotangent, *weights, *vectors)


def lanes(block):
    folded = block[:, 0:128]
    for c in range(128, block.shape[1], 128):
        folded = folded + block[:, c : c + 128]
    return folded


def backward_kernel(
    groups,
    plane,
    seq_len,
    result_ref,
    cot_any,
    cots_any,
    placed_any,
    mid_low_any,
    normed1_any,
    normed2_any,
    invs_any,
    active_any,
    slope_any,
    qkv_any,
    expo_any,
    inv_any,
    ctx_any,
    toks_any,
    wq_any,
    inter_any,
    back_t_any,
    out_t_any,
    vecs_any,
    result_out,
    gtok_out,
    grest_out,
    gqkv_out,
    vecs_ref,
    invs_ref,
    back_t,
    inter_ref,
    out_t,
    cots_ref,
    normed1_ref,
    normed2_ref,
    qkv_ref,
    expo_ref,
    inv_ref,
    ctx_ref,
    toks_ref,
    seq_sem,
    wq_ref,
    placed_ref,
    mid_low_ref,
    active_ref,
    load_sem,
    grads,
    ffn,
    branch,
    inner,
    sums,
    stack,
    acc,
    acc_q,
    pair_got,
    plane_got,
    group_sent,
    group_got,
    total_rest,
    pair_sent_q,
    pair_got_q,
    plane_got_q,
    group_sent_q,
    group_got_q,
    total_q,
    local_sem,
    result_send,
    result_recv,
    gtok_send,
    gtok_recv,
    pair_send,
    pair_recv,
    plane_send,
    plane_recv,
    group_send,
    group_recv,
    spread_send,
    spread_recv,
    join_send,
    join_recv,
    fused_from=None,
    arrived=None,
):
    fused = fused_from is not None
    gctx = cots_ref
    width, span = gctx.shape[1:]
    seqs = span // seq_len
    wide = groups * width
    hidden = inner.shape[1]
    heads = width // HEAD_DIM
    blocks = span // BLOCK
    last = blocks + groups * seqs - 1
    step = pl.program_id(0) - (fused_from or 0)
    me, at_plane = lax.axis_index("grp"), lax.axis_index("seq")
    side, pair = lax.rem(at_plane, 2), lax.div(at_plane, 2)
    group_device = [{"grp": xor(me, j, groups)} for j in range(groups)]
    pair_device = [{"seq": xor(at_plane, 2 * k, plane.size)} for k in range(plane.pairs)]
    partner = {"seq": xor(at_plane, 1, plane.size)}
    others, mates = range(1, groups), range(1, plane.pairs)

    seq_loads = (0, 1) if fused else range(4)
    loads = [] if fused else [
        (vecs_any, vecs_ref),
        (invs_any, invs_ref),
        (back_t_any, back_t),
        (inter_any, inter_ref),
        (out_t_any, out_t),
        (wq_any, wq_ref),
        (inv_any, inv_ref),
        (placed_any, placed_ref),
        (mid_low_any, mid_low_ref),
        (active_any, active_ref),
    ]

    def load(i):
        return pltpu.make_async_copy(*loads[i], load_sem.at[i])

    away = pl.ds(1, groups - 1)
    block_loads = [] if fused else [
        (cots_any.at[away], cots_ref.at[away]),
        (normed2_any, normed2_ref),
        (slope_any, inner),
        (normed1_any, normed1_ref),
        (cot_any, cots_ref.at[0]),
    ]

    def load_block(i, b):
        part = pl.ds(b * BLOCK, BLOCK)
        source, target = block_loads[i]
        sem = load_sem.at[len(loads) + i * blocks + b]
        if i == 4:
            own = ds(me * span + b * BLOCK, BLOCK, BLOCK)
            return pltpu.make_async_copy(source.at[:, own], target.at[:, part], sem)
        return pltpu.make_async_copy(source.at[:, :, part], target.at[:, :, part], sem)

    def load_seq(i, order):
        j, s, slot = groups - 1 - order // seqs, order % seqs, order % 2
        part = pl.ds(s * seq_len, seq_len)
        source, target = (
            (qkv_any.at[j, :, part], qkv_ref),
            (expo_any.at[j * seqs + s], expo_ref),
            (ctx_any.at[j, :, part], ctx_ref),
            (toks_any.at[j, :, part], toks_ref),
        )[i]
        return pltpu.make_async_copy(source, target.at[slot], seq_sem.at[i, order])

    def result_copy(j):
        mine = result_out.at[:, ds(me * span, span, span)]
        return remote(
            result_ref.at[j], mine, result_send.at[j], result_recv.at[j], group_device[j]
        )

    def result_landing(j):
        there = result_out.at[:, ds(xor(me, j, groups) * span, span, span)]
        return remote(there, there, result_send.at[j], result_recv.at[j], group_device[j])

    def gtok_copy(j, s):
        mine = gtok_out.at[:, ds(me * span + s * seq_len, seq_len, seq_len)]
        block = gctx.at[j, :, ds(s * seq_len, seq_len, seq_len)]
        if j == 0:
            return pltpu.make_async_copy(block, mine, local_sem.at[1 + s])
        return remote(block, mine, gtok_send.at[j, s], gtok_recv.at[j, s], group_device[j])

    def gtok_landing(j, s):
        start = xor(me, j, groups) * span + s * seq_len
        there = gtok_out.at[:, ds(start, seq_len, seq_len)]
        return remote(there, there, gtok_send.at[j, s], gtok_recv.at[j, s], group_device[j])

    def buffers(number):
        if number == 0:
            return (
                acc,
                acc,
                pair_got,
                plane_got,
                group_sent,
                group_got,
                total_rest,
                pl.ds(0, groups),
            )
        return (
            acc_q,
            pair_sent_q,
            pair_got_q,
            plane_got_q,
            group_sent_q,
            group_got_q,
            total_q,
            pl.ds(number - 1, 1),
        )

    def pair_copy(number):
        full, sent, got, *_, lead = buffers(number)
        half = full.shape[2] // 2
        there = ds((1 - side) * half, half, 128) if number == 0 else pl.ds(0, half)
        return remote(
            sent.at[lead, :, there],
            got.at[lead, :, pl.ds(0, half)],
            pair_send.at[number],
            pair_recv.at[number],
            partner,
        )

    def piece_of(ref, index):
        down, along, size = plane.piece(index, ref.shape[2])
        return ds(down, plane.rows, 16), ds(along, size, 128)

    def plane_copy(number, k):
        _, _, sent, got, *_, lead = buffers(number)
        down, along = piece_of(sent, xor(pair, k, plane.pairs))
        return remote(
            sent.at[lead, down, along],
            got.at[k, lead],
            plane_send.at[number, k],
            plane_recv.at[number, k],
            pair_device[k],
        )

    def group_copy(number, j):
        sent, got = buffers(number)[4:6]
        return remote(
            sent.at[j],
            got.at[j],
            group_send.at[number, j],
            group_recv.at[number, j],
            group_device[1 if j == 3 else j],
        )

    def total_piece(total, index):
        half = total.shape[1] // 2
        down, along, size = plane.piece(index, half)
        return total.at[ds(down, plane.rows, 16), ds(side * half + along, size, 128)]

    def spread_copy(number, k, index):
        part = total_piece(buffers(number)[6], index)
        return remote(
            part, part, spread_send.at[number, k], spread_recv.at[number, k], pair_device[k]
        )

    def join_copy(number, s):
        total = buffers(number)[6]
        half = total.shape[1] // 2
        part = total.at[:, ds(s * half, half, 128)]
        return remote(part, part, join_send.at[number], join_recv.at[number], partner)

    def start_pair(number):
        full, sent, *_, lead = buffers(number)
        half = full.shape[2] // 2
        if number:
            sent[lead, :, 0:half] = full[lead, :, ds((1 - side) * half, half, 128)].astype(LOW)
        pair_copy(number).start()

    def start_plane(number):
        full, _, got, *_, lead = buffers(number)
        half = full.shape[2] // 2
        pair_copy(number).wait_recv()
        summed = full[lead, :, ds(side * half, half, 128)].astype(F32)
        summed = summed + got[lead, :, 0:half].astype(F32)
        got[lead, :, 0:half] = summed.astype(LOW)
        in_plane(side, plane.pairs, lambda k: plane_copy(number, k).start())

    def plane_sum(number):
        _, _, held, got, *_, lead = buffers(number)
        for k in mates:
            plane_copy(number, k).wait_recv()
        down, along = piece_of(held, pair)
        summed = held[lead, down, along].astype(F32)
        for k in mates:
            summed = summed + got[k, lead].astype(F32)
        return summed

    def start_group(number):
        summed = plane_sum(number)
        sent, got = buffers(number)[4:6]
        if number == 0:
            for j in range(groups):
                sent[j] = summed[j].astype(LOW)
            group_copy(0, 3).start()
            group_copy(0, 1).start()
            return
        j, summed = number - 1, summed[0]
        if j == 2:
            group_copy(1, 3).wait_recv()
            summed = summed + got[3].astype(F32)
        sent[j] = summed.astype(LOW)
        group_copy(1, j).start()

    def hand_on():
        group_copy(0, 3).wait_recv()
        group_sent[2] = (group_sent[2].astype(F32) + group_got[3].astype(F32)).astype(LOW)
        group_copy(0, 2).start()

    def start_spread(number, summed):
        got, total = buffers(number)[5:7]
        for j in (1, 2):
            group_copy(number, j).wait_recv()
            summed = summed + got[j].astype(F32)
        total_piece(total, pair)[...] = summed.astype(LOW)
        in_plane(side, plane.pairs, lambda k: spread_copy(number, k, pair).start())

    def start_join(number):
        for k in mates:
            spread_copy(number, k, xor(pair, k, plane.pairs)).wait_recv()
        join_copy(number, side).start()

    @pl.when(step == 0)
    def _():
        if not fused:
            greet(group_device[1:] + pair_device[1:] + [partner])
            for i in range(3):
                load(i).start()
            for i in range(len(block_loads)):
                load_block(i, 0).start()
            for i in (3, 4):
                load(i).start()
            meet(group_device[1:] + pair_device[1:] + [partner])
        in_turn(me, lambda j: result_copy(j).start())
        for b in range(1, blocks):
            for i in range(len(block_loads)):
                load_block(i, b).start()
        for i in range(0 if fused else 5, len(loads)):
            load(i).start()
        for i in seq_loads:
            load_seq(i, 0).start()
        for ref in (acc_q, sums):
            ref[...] = jnp.zeros_like(ref)
        for i in () if fused else range(5):
            load(i).wait()

    for b in range(blocks):

        @pl.when(step == b)
        def _():
            for i in range(len(block_loads)):
                load_block(i, b).wait()
            if fused:
                arrived(b)

    for order in range(groups * seqs):

        @pl.when(step == blocks + order)
        def _():
            for i in seq_loads:
                load_seq(i, order).wait()
                if order + 1 < groups * seqs:
                    load_seq(i, order + 1).start()

    @pl.when((step >= 0) & (step < blocks))
    def _():
        at = ds(step * BLOCK, BLOCK, BLOCK)

        def column(group, which):
            return vecs_ref[group, :, which : which + 1]

        inv1, inv2 = invs_ref[0:1, at], invs_ref[1:2, at]
        zero = jnp.zeros((1, BLOCK), F32)
        first, second = zero, zero
        for j in range(groups):
            rows = cots_ref[j, :, at].astype(F32)
            normed = normed2_ref[j, :, at].astype(F32)
            scaled = rows * column(j, GAIN2)
            first += jnp.sum(scaled, axis=0, keepdims=True)
            second += jnp.sum(scaled * normed, axis=0, keepdims=True)
            sums[GAIN2 - B_OUT, j] += lanes(rows * normed)
            sums[SHIFT2 - B_OUT, j] += lanes(rows)
        first, second = first * (1.0 / wide), second * (1.0 / wide)
        next_first, next_second = zero, zero
        for j in range(groups):
            scaled = cots_ref[j, :, at].astype(F32) * column(j, GAIN2)
            rows = inv2 * (scaled - first - normed2_ref[j, :, at].astype(F32) * second)
            low_rows = rows.astype(LOW)
            sums[B_BACK - B_OUT, j] += lanes(low_rows.astype(F32))
            ffn[j, :, at] = low_rows
            for a in range(0, hidden, width):
                inner[j, a : a + width, at] = (
                    mm(back_t[j, a : a + width, :], low_rows).astype(LOW)
                    * inner[j, a : a + width, at]
                )
            rows = rows + mm(inter_ref[j], inner[j, :, at])
            normed = normed1_ref[j, :, at].astype(F32)
            sums[GAIN1 - B_OUT, j] += lanes(rows * normed)
            sums[SHIFT1 - B_OUT, j] += lanes(rows)
            scaled = rows * column(j, GAIN1)
            next_first += jnp.sum(scaled, axis=0, keepdims=True)
            next_second += jnp.sum(scaled * normed, axis=0, keepdims=True)
            grads[j] = scaled
        first, second = next_first * (1.0 / wide), next_second * (1.0 / wide)
        for j in range(groups):
            rows = inv1 * (grads[j] - first - normed1_ref[j, :, at].astype(F32) * second)
            low_rows = rows.astype(LOW)
            branch[j * width : (j + 1) * width, at] = low_rows
            sums[0, j] += lanes(low_rows.astype(F32))
        for j in range(groups):
            there = ds(xor(me, j, groups) * width, width, width)
            gctx[j, :, at] = mm(out_t[there, :], branch[:, at]).astype(LOW)

    @pl.when(step == blocks - 1)
    def _():
        for i in range(0 if fused else 5, len(loads)):
            load(i).wait()
        lane = lax.broadcasted_iota(jnp.int32, (width, 128), 1)
        ones = jnp.ones((16, span), LOW)
        for j in range(groups):
            rows = slice(j * width, (j + 1) * width)
            acc[j, :, 0:wide] = mm_nt(branch[rows, :], placed_ref[...]).astype(LOW)
            both = mm_nt(jnp.concatenate([mid_low_ref[j], ones], axis=0), inner[j])
            acc[j, :, wide : wide + hidden] = both[0:width].astype(LOW)
            acc[j, :, wide + hidden : wide + 2 * hidden] = mm_nt(ffn[j], active_ref[j]).astype(LOW)
            small = jnp.zeros((width, 128), F32)
            for which in (B_OUT, GAIN1, SHIFT1, B_BACK, GAIN2, SHIFT2):
                added = jnp.sum(sums[which - B_OUT, j], axis=1, keepdims=True)
                small = jnp.where(lane == which, added, small)
            for a in range(0, hidden, width):
                added = both[width : width + 8, a : a + width].T[:, 0:1]
                small = jnp.where(lane == B_INTER + a // width, added, small)
            acc[j, :, wide + 2 * hidden : wide + 2 * hidden + 128] = small.astype(LOW)
        if acc.shape[2] > wide + 2 * hidden + 128:
            acc[:, :, wide + 2 * hidden + 128 :] = jnp.zeros_like(acc[:, :, wide + 2 * hidden + 128 :])
        start_pair(0)

    @pl.when(step >= blocks)
    def _():
        order = step - blocks
        j, s, slot = groups - 1 - lax.div(order, seqs), lax.rem(order, seqs), lax.rem(order, 2)
        at = ds(s * seq_len, seq_len, seq_len)
        row = lax.broadcasted_iota(jnp.int32, (16, seq_len), 0)
        minus_rows = jnp.where(row < 3, -1.0, 0.0).astype(LOW)
        chunks = [(h, c) for h in range(heads) for c in range(0, seq_len, BLOCK)]

        def context_of(low, top):
            if fused:
                start = xor(me, j, groups) * width + low
                return placed_ref[ds(start, HEAD_DIM, HEAD_DIM), at]
            return ctx_ref[slot, low:top, :]

        def head(h):
            low, top = h * HEAD_DIM, (h + 1) * HEAD_DIM
            values = jnp.concatenate(
                [qkv_ref[slot, 2 * width + low : 2 * width + top, :], minus_rows], axis=0
            )
            scaled = (gctx[j, low:top, at].astype(F32) * inv_ref[j, h : h + 1, at]).astype(LOW)
            delta = jnp.sum(
                scaled.astype(F32) * context_of(low, top).astype(F32), axis=0, keepdims=True
            )
            first = delta.astype(LOW).astype(F32)
            second = (delta - first).astype(LOW).astype(F32)
            third = delta - first - second
            parts = jnp.where(
                row == 0, first, jnp.where(row == 1, second, jnp.where(row == 2, third, 0.0))
            ).astype(LOW)
            return values.T, scaled, jnp.concatenate([scaled, parts], axis=0)

        made = [head(0)]

        def shifted_of(h, c):
            if h == len(made):
                made.append(head(h))
            return mm(made[h][0], made[h][2][:, c : c + BLOCK])

        ready = shifted_of(*chunks[0])
        for i, (h, c) in enumerate(chunks):
            shifted = ready
            if i + 1 < len(chunks):
                ready = shifted_of(*chunks[i + 1])
            low, top = h * HEAD_DIM, (h + 1) * HEAD_DIM
            part = slice(c, c + BLOCK)
            expo = expo_ref[slot, h, :, part]
            grad_s = expo * shifted.astype(LOW)
            add_k = mm_nt(qkv_ref[slot, low:top, part], grad_s)
            add_v = mm_nt(made[h][1][:, part], expo)
            grad_k = add_k if c == 0 else grad_k + add_k
            grad_v = add_v if c == 0 else grad_v + add_v
            stack[low:top, part] = (
                mm(qkv_ref[slot, width + low : width + top, :], grad_s) * (1.0 / math.sqrt(HEAD_DIM))
            ).astype(LOW)
            if c + BLOCK == seq_len:
                stack[width + low : width + top, :] = grad_k.astype(LOW)
                stack[2 * width + low : 2 * width + top, :] = grad_v.astype(LOW)
        rows = stack[...]
        gctx[j, :, at] = (
            branch[ds(j * width, width, width), at].astype(F32) + mm_tn(wq_ref[j], rows)
        ).astype(LOW)
        acc_q[j, :, 0 : 3 * width] += mm_nt(toks_ref[j, :, at] if fused else toks_ref[slot], rows)
        added = jnp.sum(rows.astype(F32), axis=1, keepdims=True)
        lane = lax.broadcasted_iota(jnp.int32, (width, 128), 1)
        acc_q[j, :, 3 * width : 3 * width + 128] += jnp.where(
            lane == B_QUERY, added[0:width], jnp.where(lane == B_VALUE, added[2 * width :], 0.0)
        )

    middle = (me == 1) | (me == 2)

    def outer_sends(j, s):
        pl.when(jnp.logical_not(middle))(lambda: gtok_copy(j, s).start())

    def middle_sends(first, second):
        for core, pieces in ((0, first), (1, second)):

            @pl.when(middle & (side == core))
            def _():
                for j, s in pieces:
                    gtok_copy(j, s).start()

    def first_step():
        outer_sends(3, 0)
        start_plane(0)

    def second_step():
        outer_sends(3, 1)
        start_pair(4)

    def third_step():
        outer_sends(2, 0)
        start_plane(4)

    def fourth_step():
        outer_sends(2, 1)
        start_pair(3)

    def fifth_step():
        middle_sends([(3, 0)], [(3, 0)])
        start_plane(3)

    def sixth_step():
        start_group(0)
        middle_sends([(1, 0)], [(3, 1)])
        start_pair(2)
        start_group(4)

    def seventh_step():
        hand_on()
        start_plane(2)
        start_group(3)
        outer_sends(1, 0)
        outer_sends(1, 1)
        middle_sends([(1, 1)], [(2, 0)])
        gtok_copy(0, 0).start()

    def eighth_step():
        start_pair(1)
        start_group(2)
        middle_sends([(3, 1), (2, 0), (2, 1)], [(2, 1), (1, 0), (1, 1)])
        gtok_copy(0, 1).start()

    for order, finish_step in enumerate(
        (
            first_step,
            second_step,
            third_step,
            fourth_step,
            fifth_step,
            sixth_step,
            seventh_step,
            eighth_step,
        )
    ):
        pl.when(step == blocks + order)(finish_step)

    @pl.when(step == last)
    def _():
        start_plane(1)
        start_spread(0, group_sent[0].astype(F32))
        start_spread(1, plane_sum(1)[0])
        start_join(0)
        start_join(1)
        join_copy(0, 1 - side).wait_recv()
        rest_done = pltpu.make_async_copy(total_rest, grest_out, local_sem.at[1 + seqs])
        rest_done.start()
        join_copy(1, 1 - side).wait_recv()
        q_done = pltpu.make_async_copy(total_q, gqkv_out, local_sem.at[2 + seqs])
        q_done.start()
        for s in range(seqs):
            gtok_copy(0, s).wait()
        for j in others:
            result_copy(j).wait_send()
            result_landing(j).wait_recv()
            for s in range(seqs):
                gtok_copy(j, s).wait_send()
                gtok_landing(j, s).wait_recv()
            for number in (0, 1):
                group_copy(number, j).wait_send()
        for number in range(1 + groups):
            pair_copy(number).wait_send()
            for k in mates:
                plane_copy(number, k).wait_send()
        for number in (0, 1):
            for k in mates:
                spread_copy(number, k, pair).wait_send()
            join_copy(number, side).wait_send()
        rest_done.wait()
        q_done.wait()


def sum_buffers(groups, width, plane, columns):
    half = columns // 2
    size = half // plane.col_parts
    return [
        pltpu.VMEM((groups, width, half), LOW),
        pltpu.VMEM((plane.pairs, groups, plane.rows, size), LOW),
        pltpu.VMEM((groups, plane.rows, size), LOW),
        pltpu.VMEM((groups, plane.rows, size), LOW),
        pltpu.VMEM((width, columns), LOW),
    ]


def sum_semaphores(groups, seqs, plane):
    dma = pltpu.SemaphoreType.DMA
    numbers = 1 + groups
    shapes = [(3 + seqs,)] + [(groups,)] * 2 + [(groups, seqs)] * 2 + [(numbers,)] * 2
    shapes += [(numbers, plane.pairs)] * 2 + [(2, groups)] * 2 + [(2, plane.pairs)] * 2 + [(2,)] * 2
    return [dma(shape) for shape in shapes]


def backward(sizes, cotangent, made):
    groups, plane, seq_len, hidden = sizes
    cots, toks, wq, inter, back_t, out_t, vecs, placed, result, mid_low, normed1, normed2 = made[0:12]
    active, slope, qkv, expo, inv, ctx, invs = made[12:]
    width, span = toks.shape[1:]
    seqs, heads, wide = span // seq_len, width // HEAD_DIM, groups * width
    blocks, attention = span // BLOCK, groups * seqs
    columns = plane.padded(wide + 2 * hidden + 128)
    columns_q = plane.padded(3 * width + 128)
    anywhere = pl.BlockSpec(memory_space=pl.ANY)

    def low(*shape):
        return jax.ShapeDtypeStruct(shape, LOW)

    dma = pltpu.SemaphoreType.DMA
    return pl.pallas_call(
        functools.partial(backward_kernel, groups, plane, seq_len),
        grid=(blocks + attention,),
        in_specs=[anywhere] * 20,
        out_specs=[anywhere] * 4,
        out_shape=[
            low(width, groups * span),
            low(width, groups * span),
            low(width, columns),
            low(width, columns_q),
        ],
        scratch_shapes=[
            pltpu.VMEM(vecs.shape, F32),
            pltpu.VMEM(invs.shape, F32),
            pltpu.VMEM(back_t.shape, LOW),
            pltpu.VMEM(inter.shape, LOW),
            pltpu.VMEM(out_t.shape, LOW),
            pltpu.VMEM(cots.shape, LOW),
            pltpu.VMEM(normed1.shape, LOW),
            pltpu.VMEM(normed2.shape, LOW),
            pltpu.VMEM((2, 3 * width, seq_len), LOW),
            pltpu.VMEM((2, heads, seq_len, seq_len), LOW),
            pltpu.VMEM(inv.shape, F32),
            pltpu.VMEM((2, width, seq_len), LOW),
            pltpu.VMEM((2, width, seq_len), LOW),
            dma((4, groups * seqs)),
            pltpu.VMEM(wq.shape, LOW),
            pltpu.VMEM(placed.shape, LOW),
            pltpu.VMEM(mid_low.shape, LOW),
            pltpu.VMEM(active.shape, LOW),
            dma((10 + 5 * blocks,)),
            pltpu.VMEM((groups, width, BLOCK), F32),
            pltpu.VMEM((groups, width, span), LOW),
            pltpu.VMEM((wide, span), LOW),
            pltpu.VMEM((groups, hidden, span), LOW),
            pltpu.VMEM((B_INTER - B_OUT, groups, width, 128), F32),
            pltpu.VMEM((3 * width, seq_len), LOW),
            pltpu.VMEM((groups, width, round_up(wide + 2 * hidden + 128, 256)), LOW),
            pltpu.VMEM((groups, width, round_up(3 * width + 128, 256)), F32),
        ]
        + sum_buffers(groups, width, plane, columns)
        + [pltpu.VMEM((groups, width, columns_q // 2), LOW)]
        + sum_buffers(groups, width, plane, columns_q)
        + sum_semaphores(groups, seqs, plane),
        compiler_params=pltpu.CompilerParams(
            vmem_limit_bytes=VMEM_BYTES, collective_id=1, has_side_effects=True
        ),
        name="backward",
    )(
        result,
        cotangent,
        cots,
        placed,
        mid_low,
        normed1,
        normed2,
        invs,
        active,
        slope,
        qkv,
        expo,
        inv,
        ctx,
        toks,
        wq,
        inter,
        back_t,
        out_t,
        vecs,
    )


def fused_kernel(groups, plane, seq_len, *refs):
    refs = list(refs)

    def take(count):
        taken = refs[0:count]
        del refs[0:count]
        return taken

    len_ref, tok_ref, cot_ref = take(3)
    rest_refs, qkv_any, vector_any = take(3), take(3), take(VECTOR_COUNT)
    result_any, qkv_hbm, expo_hbm, *outs = take(7)
    toks, wq, rest, vec_rows, vecs, placed, inter_t, back_t, out_t, resid, qkv_refs = take(11)
    vector_refs = take(VECTOR_COUNT)
    result, mid_low, normed1, normed2, active, slope, cots = take(7)
    qkv_slots, expo_slots, ctx_slot, inv_all, invs = take(5)
    save_sem, local_sem, store_sem, own_sem = take(4)
    forward_sems = take(18)
    width, span = toks.shape[1:]
    seqs, wide, hidden = span // seq_len, groups * width, active.shape[1]
    steps = groups * seqs
    offset = steps + span // BLOCK
    step = pl.program_id(0)
    me = lax.axis_index("grp")

    def stores(k):
        j, s, slot = k // seqs, k % seqs, k % 2
        there = qkv_hbm.at[j, :, pl.ds(s * seq_len, seq_len)]
        return [
            pltpu.make_async_copy(qkv_slots.at[slot], there, store_sem.at[0, k]),
            pltpu.make_async_copy(expo_slots.at[slot], expo_hbm.at[k], store_sem.at[1, k]),
        ]

    own_cot = pltpu.make_async_copy(
        cot_ref.at[:, ds(me * span, span, span)], cots.at[0], own_sem.at[0]
    )
    for k in range(steps):

        @pl.when(step == k + 2)
        def _():
            for copy in stores(k):
                copy.wait()

    at_step = jnp.minimum(step, steps - 1)
    j, s = lax.div(at_step, seqs), lax.rem(at_step, seqs)
    slot = pl.ds(lax.rem(at_step, 2), 1)
    block = jnp.minimum(jnp.maximum(step - steps, 0), span // BLOCK - 1)
    cots_here, all_saved, all_sent = forward_steps(
        groups,
        plane,
        seq_len,
        len_ref,
        tok_ref,
        cot_ref,
        rest_refs,
        qkv_any,
        vector_any,
        (cots,) + (None,) * 7,
        (result_any,) + (None,) * 5,
        (
            qkv_slots.at[slot],
            expo_slots.at[slot],
            inv_all.at[pl.ds(j, 1), :, ds(s * seq_len, seq_len, seq_len)],
            ctx_slot,
            invs.at[:, ds(block * BLOCK, BLOCK, BLOCK)],
        ),
        (result, mid_low, normed1, normed2, active, slope, save_sem),
        (toks, wq, rest, vec_rows, vecs, placed, inter_t, back_t, out_t, resid),
        qkv_refs,
        vector_refs,
        local_sem,
        *forward_sems,
        fused=True,
    )
    for k in range(steps):

        @pl.when(step == k)
        def _():
            for copy in stores(k):
                copy.start()

    pl.when(step == 1)(own_cot.start)

    pl.when(step == offset)(all_saved)

    def arrived(b):
        per_seq = seq_len // BLOCK
        if b == 0:
            own_cot.wait()
        if b % per_seq == 0:
            cots_here(b // per_seq)

    backward_kernel(
        groups,
        plane,
        seq_len,
        result_any,
        *(None,) * 9,
        qkv_hbm,
        expo_hbm,
        None,
        qkv_hbm,
        qkv_hbm,
        *(None,) * 5,
        *outs,
        vecs,
        invs,
        back_t,
        rest.at[:, :, pl.ds(wide, hidden)],
        out_t,
        cots,
        normed1,
        normed2,
        qkv_slots,
        expo_slots,
        inv_all,
        ctx_slot,
        toks,
        take(1)[0],
        wq.at[:, pl.ds(0, 3 * width), :],
        placed,
        mid_low,
        active,
        None,
        resid,
        result,
        take(1)[0],
        slope,
        *refs,
        fused_from=offset,
        arrived=arrived,
    )
    pl.when(step == offset + span // BLOCK + steps - 1)(all_sent)


def fused(sizes, lengths, tokens, cotangent, weights, vectors):
    groups, plane, seq_len, hidden = sizes
    width, total = tokens.shape
    span = total // groups
    seqs, heads, wide = span // seq_len, width // HEAD_DIM, groups * width
    attention, blocks = groups * seqs, span // BLOCK
    wq_rows = round_up(3 * width, 16 * plane.size)
    rest_columns = plane.padded(wide + 2 * hidden)
    columns = plane.padded(wide + 2 * hidden + 128)
    columns_q = plane.padded(3 * width + 128)
    anywhere = pl.BlockSpec(memory_space=pl.ANY)
    dma = pltpu.SemaphoreType.DMA

    def low(*shape):
        return jax.ShapeDtypeStruct(shape, LOW)

    def keep(*shape):
        return pltpu.VMEM(shape, LOW)

    def keep_f32(*shape):
        return pltpu.VMEM(shape, F32)

    gate = [dma((groups,)), dma((groups,))]
    by_token, by_hidden = keep(groups, width, span), keep(groups, hidden, span)
    forward_scratch = [
        by_token,
        keep(groups, wq_rows, width),
        keep(groups, width, rest_columns),
        keep_f32(groups, VECTORS, round_up(width, 128)),
        keep_f32(groups, width, 128),
        keep(wide, span),
        keep(groups, hidden, width),
        keep(groups, hidden, width),
        keep(wide, wide),
        keep_f32(groups, width, BLOCK),
        keep(3, width, width),
    ]
    forward_scratch += [keep_f32(*vector.shape) for vector in vectors]
    forward_scratch += [by_token] * 4 + [by_hidden] * 2 + [by_token]
    forward_scratch += [
        keep(2, 3 * width, seq_len),
        keep(2, heads, seq_len, seq_len),
        keep(1, width, seq_len),
        keep_f32(groups, 8, span),
        keep_f32(8, span),
        dma((6, blocks)),
        dma((14 + VECTOR_COUNT,)),
        dma((2, attention)),
        dma((1,)),
    ]
    forward_scratch += [dma((groups, seqs))] * 4 + gate
    forward_scratch += gate + [dma((2, plane.pairs)), dma((2, plane.pairs)), dma((2,)), dma((2,))]
    forward_scratch += gate + [dma((plane.pairs,)), dma((plane.pairs,)), dma((1,)), dma((1,))]
    backward_scratch = [
        dma((4, attention)),
        keep(wide, span),
        keep_f32(B_INTER - B_OUT, groups, width, 128),
        keep(3 * width, seq_len),
        keep(groups, width, round_up(wide + 2 * hidden + 128, 256)),
        keep_f32(groups, width, round_up(3 * width + 128, 256)),
    ]
    backward_scratch += sum_buffers(groups, width, plane, columns)
    backward_scratch += [keep(groups, width, columns_q // 2)]
    backward_scratch += sum_buffers(groups, width, plane, columns_q)
    backward_scratch += sum_semaphores(groups, seqs, plane)
    return pl.pallas_call(
        functools.partial(fused_kernel, groups, plane, seq_len),
        grid=(2 * (attention + blocks),),
        in_specs=[pl.BlockSpec(memory_space=pltpu.SMEM)] + [anywhere] * (8 + VECTOR_COUNT),
        out_specs=[anywhere] * 7,
        out_shape=[
            low(groups, width, span),
            low(groups, 3 * width, span),
            low(attention, heads, seq_len, seq_len),
            low(width, total),
            low(width, total),
            low(width, columns),
            low(width, columns_q),
        ],
        scratch_shapes=forward_scratch + backward_scratch,
        compiler_params=pltpu.CompilerParams(
            vmem_limit_bytes=VMEM_BYTES, collective_id=2, has_side_effects=True
        ),
        name="layer",
    )(lengths, tokens, cotangent, *weights, *vectors)


FINISH_PARTS = 4


def finish_kernel(groups, hidden, own_ref, result_ref, gtok_ref, rest_ref, qkv_ref, *refs):
    outs, refs = refs[0:17], refs[17:]
    result, gtok_low, gtok, rest, qkv, *made, in_sem, out_sem = refs
    width, rows = result_ref.shape
    wide, part, span = groups * width, width // FINISH_PARTS, rows // groups
    me = lax.axis_index("grp")
    made = dict(zip(range(2, 17), made))

    def load(i):
        if i < FINISH_PARTS:
            piece = pl.ds(i * part, part)
            return pltpu.make_async_copy(gtok_ref.at[piece], gtok_low.at[piece], in_sem.at[i])
        if i < FINISH_PARTS + 2:
            source, target = ((rest_ref, rest), (qkv_ref, qkv))[i - FINISH_PARTS]
            return pltpu.make_async_copy(source, target, in_sem.at[i])
        j = i - FINISH_PARTS - 2
        columns = ds(xor(me, j, groups) * span, span, span)
        source = result_ref.at[:, columns] if j else own_ref.at[0]
        return pltpu.make_async_copy(source, result.at[:, columns], in_sem.at[i])

    def store(i):
        return pltpu.make_async_copy(made[i], outs[i], out_sem.at[i])

    def store_tokens(i):
        piece = pl.ds(i * part, part)
        return pltpu.make_async_copy(gtok.at[piece], outs[1].at[piece], out_sem.at[17 + i])

    whole = pltpu.make_async_copy(result, outs[0], out_sem.at[0])
    for i in range(FINISH_PARTS + 2 + groups):
        load(i).start()
    for i in range(FINISH_PARTS):
        piece = pl.ds(i * part, part)
        load(i).wait()
        gtok[piece, :] = gtok_low[piece, :].astype(F32)
        store_tokens(i).start()
    load(FINISH_PARTS).wait()
    load(FINISH_PARTS + 1).wait()
    for i in range(3):
        made[2 + i][...] = qkv[:, i * width : (i + 1) * width].astype(F32)
    small = qkv[:, 3 * width : 3 * width + 128].astype(F32).T
    made[5][...] = small[B_QUERY : B_QUERY + 1]
    made[6][...] = small[B_VALUE : B_VALUE + 1]
    made[7][...] = rest[:, 0:wide].astype(F32)
    made[11][...] = rest[:, wide : wide + hidden].astype(F32)
    made[13][...] = rest[:, wide + hidden : wide + 2 * hidden].astype(F32)
    small = rest[:, wide + 2 * hidden : wide + 2 * hidden + 128].astype(F32).T
    for i, which in ((8, B_OUT), (9, GAIN1), (10, SHIFT1), (14, B_BACK), (15, GAIN2), (16, SHIFT2)):
        made[i][...] = small[which : which + 1]
    row = jnp.concatenate(
        [small[B_INTER + a : B_INTER + a + 1] for a in range(hidden // width)], axis=1
    )
    for i in range(hidden // 128):
        made[12][i : i + 1, :] = row[:, i * 128 : (i + 1) * 128]
    for i in range(2, 17):
        store(i).start()
    for j in range(groups):
        load(FINISH_PARTS + 2 + j).wait()
    whole.start()
    for i in range(FINISH_PARTS):
        store_tokens(i).wait()
    for i in range(2, 17):
        store(i).wait()
    whole.wait()


def finish(sizes, own, result, grad_tokens, grad_rest, grad_qkv):
    groups, _, _, hidden = sizes
    width, rows = result.shape
    matrix, vector = (width, groups * width), (1, width)
    shapes = [(width, width)] * 3 + [vector] * 2 + [matrix] + [vector] * 3
    shapes += [(width, hidden), (hidden // 128, 128), (width, hidden)] + [vector] * 3
    anywhere = pl.BlockSpec(memory_space=pl.ANY)
    return pl.pallas_call(
        functools.partial(finish_kernel, groups, hidden),
        in_specs=[anywhere] * 5,
        out_specs=[anywhere] * 17,
        out_shape=[jax.ShapeDtypeStruct((width, rows), LOW), jax.ShapeDtypeStruct((width, rows), F32)]
        + [jax.ShapeDtypeStruct(shape, F32) for shape in shapes],
        scratch_shapes=[
            pltpu.VMEM((width, rows), LOW),
            pltpu.VMEM((width, rows), LOW),
            pltpu.VMEM((width, rows), F32),
            pltpu.VMEM(grad_rest.shape, LOW),
            pltpu.VMEM(grad_qkv.shape, LOW),
        ]
        + [pltpu.VMEM(shape, F32) for shape in shapes]
        + [
            pltpu.SemaphoreType.DMA((FINISH_PARTS + 2 + groups,)),
            pltpu.SemaphoreType.DMA((17 + FINISH_PARTS,)),
        ],
        compiler_params=pltpu.CompilerParams(vmem_limit_bytes=VMEM_BYTES),
        name="finish",
    )(own, result, grad_tokens, grad_rest, grad_qkv)


def joined(halves, columns):
    half, whole = round_up(columns, 256) // 2, halves.shape[1]
    if 2 * half == whole:
        return halves
    return jnp.concatenate([halves[:, 0:half], halves[:, whole // 2 : whole // 2 + half]], axis=1)


def local(
    tokens,
    cotangent,
    lengths,
    w_query,
    w_key,
    w_value,
    b_query,
    b_value,
    w_out,
    b_out,
    gain_attn,
    shift_attn,
    w_inter,
    b_inter,
    w_back,
    b_back,
    gain_ffn,
    shift_ffn,
):
    width, rows = tokens.shape
    groups = lax.axis_size("grp")
    plane = Plane(lax.axis_size("seq"), width)
    seq_len = rows // lengths.shape[0]
    hidden = w_inter.shape[1]
    wide = groups * width
    sizes = (groups, plane, seq_len, hidden)

    vectors = [b_query, b_value, b_out, gain_attn, shift_attn, b_back, gain_ffn, shift_ffn, b_inter]
    weights = (w_out, w_inter, w_back, w_query, w_key, w_value)
    vectors = [vector.reshape(1, -1) for vector in vectors[:-1]] + [b_inter.reshape(-1, 128)]
    if plane.size == 8:
        own, _, _, *made = fused(sizes, lengths, tokens, cotangent, weights, vectors)
    else:
        saved = forward(sizes, lengths, tokens, cotangent, weights, vectors)
        own, made = saved[8], backward(sizes, cotangent, saved)
    result, grad_tokens, grad_rest, grad_qkv = made
    grad_rest = joined(grad_rest, wide + 2 * hidden + 128)
    grad_qkv = joined(grad_qkv, 3 * width + 128)
    outs = finish(sizes, own, result, grad_tokens, grad_rest, grad_qkv)
    return tuple(out.reshape(-1) if out.shape[0] < 8 else out for out in outs)


def solution(mesh):
    flat, matrix, vector = P("grp", "seq"), P("grp", None), P("grp")
    return jax.shard_map(
        local,
        mesh=mesh,
        in_specs=(flat, flat, P("seq"), matrix, matrix, matrix, vector, vector, matrix)
        + (vector, vector, vector, matrix, vector, matrix, vector, vector, vector),
        out_specs=(flat, flat, matrix, matrix, matrix, vector, vector, matrix, vector)
        + (vector, vector, matrix, vector, matrix, vector, vector, vector),
        check_vma=False,
    )
```

```python
import functools
import math

import jax
import jax.numpy as jnp
from jax import lax
from jax.experimental import pallas as pl
from jax.experimental.pallas import tpu as pltpu
from jax.sharding import PartitionSpec as P

HEAD_DIM = 64
EPS = 1e-12
MASKED = -1e30
F32, LOW = jnp.float32, jnp.bfloat16
VMEM_BYTES = 60 * 1024 * 1024
MESH = pl.DeviceIdType.MESH
BLOCK = 256
ERF_P = 0.3275911
ERF_A = (0.254829592, -0.284496736, 1.421413741, -1.453152027, 1.061405429)
B_QUERY, B_VALUE, B_OUT, GAIN1, SHIFT1, B_BACK, GAIN2, SHIFT2, B_INTER = range(9)
VECTORS, VECTOR_COUNT = 16, 9


def mm(left, right):
    return jnp.dot(left, right, preferred_element_type=F32)


def mm_tn(left, right):
    return lax.dot_general(left, right, (((0,), (0,)), ((), ())), preferred_element_type=F32)


def mm_nt(left, right):
    return lax.dot_general(left, right, (((1,), (1,)), ((), ())), preferred_element_type=F32)


def round_up(value, unit):
    return -(-value // unit) * unit


def bit(value, unit):
    if isinstance(value, int):
        return value // unit % 2
    return lax.rem(lax.div(value, jnp.int32(unit)), jnp.int32(2))


def xor(left, right, size):
    total, unit = 0, 1
    while unit < size:
        total = total + unit * ((bit(left, unit) + bit(right, unit)) % 2)
        unit *= 2
    return total


class Plane:
    def __init__(self, size, rows):
        self.size, self.pairs = size, size // 2
        self.row_parts = min(4, self.pairs)
        self.col_parts = self.pairs // self.row_parts
        self.rows = rows // self.row_parts

    def padded(self, columns):
        return 2 * round_up(round_up(columns, 256) // 2, 128 * self.col_parts)

    def piece(self, index, columns):
        width = columns // self.col_parts
        down, along = lax.rem(index, self.row_parts), lax.div(index, self.row_parts)
        if self.col_parts == 1:
            along = 0
        return down * self.rows, along * width, width


def ds(start, size, unit):
    return pl.ds(start if isinstance(start, int) else pl.multiple_of(start, unit), size)


def remote(src, dst, send, recv, device):
    return pltpu.make_async_remote_copy(
        src_ref=src, dst_ref=dst, send_sem=send, recv_sem=recv, device_id=device, device_id_type=MESH
    )


def in_turn(me, start):
    middle = (me == 1) | (me == 2)

    @pl.when(middle)
    def _():
        for j in (2, 1, 3):
            start(j)

    @pl.when(jnp.logical_not(middle))
    def _():
        for j in (1, 2, 3):
            start(j)


def greet(devices):
    barrier = pltpu.get_barrier_semaphore()
    for device in devices:
        pl.semaphore_signal(barrier, inc=1, device_id=device, device_id_type=MESH)


def meet(devices):
    pl.semaphore_wait(pltpu.get_barrier_semaphore(), len(devices))


def in_plane(side, pairs, start):
    first = [k for k in (1, 2) if k < pairs]
    rest = range(3, pairs)

    @pl.when(side == 0)
    def _():
        for k in (*first, *rest):
            start(k)

    @pl.when(side == 1)
    def _():
        for k in (*first[::-1], *rest):
            start(k)


def gelu_parts(inner):
    below = 1.0 + (ERF_P / math.sqrt(2.0)) * jnp.abs(inner)
    t = pl.reciprocal(below, approx=True)
    t = t * (2.0 - below * t)
    bell = jnp.exp(-0.5 * inner * inner)
    poly = 0.5 * ERF_A[4]
    for coeff in ERF_A[3::-1]:
        poly = poly * t + 0.5 * coeff
    tail = poly * t * bell
    below = jnp.where(inner < 0, tail, 1.0 - tail)
    return inner * below, below + inner * bell * (1.0 / math.sqrt(2.0 * math.pi))


def forward_kernel(
    groups,
    plane,
    seq_len,
    len_ref,
    tok_ref,
    cot_ref,
    w_out_ref,
    w_inter_ref,
    w_back_ref,
    w_query_ref,
    w_key_ref,
    w_value_ref,
    *refs,
):
    vector_refs, refs = refs[0:VECTOR_COUNT], refs[VECTOR_COUNT:]
    forward_body(
        groups,
        plane,
        seq_len,
        len_ref,
        tok_ref,
        cot_ref,
        (w_out_ref, w_inter_ref, w_back_ref),
        (w_query_ref, w_key_ref, w_value_ref),
        vector_refs,
        *refs,
    )


def forward_body(
    groups,
    plane,
    seq_len,
    len_ref,
    tok_ref,
    cot_ref,
    rest_refs,
    qkv_any,
    vector_any,
    cots_out,
    toks_out,
    wq_out,
    inter_out,
    back_t_out,
    out_t_out,
    vecs_out,
    placed_out,
    result_out,
    mid_low_out,
    normed1_out,
    normed2_out,
    active_out,
    slope_out,
    qkv_ref,
    expo_ref,
    inv_ref,
    ctx_ref,
    invs_ref,
    result_ref,
    mid_low_ref,
    normed1_ref,
    normed2_ref,
    active_ref,
    slope_ref,
    save_sem,
    toks,
    wq,
    rest,
    vec_rows,
    vecs,
    placed,
    inter_t,
    back_t,
    out_t,
    resid,
    qkv_refs,
    *rest_of_scratch,
):
    vector_refs = rest_of_scratch[0:VECTOR_COUNT]
    forward_steps(
        groups,
        plane,
        seq_len,
        len_ref,
        tok_ref,
        cot_ref,
        rest_refs,
        qkv_any,
        vector_any,
        (cots_out, toks_out, wq_out, inter_out, back_t_out, out_t_out, vecs_out, placed_out),
        (result_out, mid_low_out, normed1_out, normed2_out, active_out, slope_out),
        (qkv_ref, expo_ref, inv_ref, ctx_ref, invs_ref),
        (result_ref, mid_low_ref, normed1_ref, normed2_ref, active_ref, slope_ref, save_sem),
        (toks, wq, rest, vec_rows, vecs, placed, inter_t, back_t, out_t, resid),
        qkv_refs,
        vector_refs,
        *rest_of_scratch[VECTOR_COUNT:],
    )


def forward_steps(
    groups,
    plane,
    seq_len,
    len_ref,
    tok_ref,
    cot_ref,
    rest_refs,
    qkv_any,
    vector_any,
    outs,
    saved_outs,
    blocked_outs,
    saved,
    scratch,
    qkv_refs,
    vector_refs,
    local_sem,
    tok_send,
    tok_recv,
    cot_send,
    cot_recv,
    vec_send,
    vec_recv,
    q1_send,
    q1_recv,
    q2_send,
    q2_recv,
    q3_send,
    q3_recv,
    r1_send,
    r1_recv,
    r2_send,
    r2_recv,
    r3_send,
    r3_recv,
    fused=False,
):
    cots_out, toks_out, wq_out, inter_out, back_t_out, out_t_out, vecs_out, placed_out = outs
    result_out, mid_low_out, normed1_out, normed2_out, active_out, slope_out = saved_outs
    qkv_ref, expo_ref, inv_ref, ctx_ref, invs_ref = blocked_outs
    result_ref, mid_low_ref, normed1_ref, normed2_ref, active_ref, slope_ref, save_sem = saved
    toks, wq, rest, vec_rows, vecs, placed, inter_t, back_t, out_t, resid = scratch
    width, span = toks.shape[1:]
    seqs = span // seq_len
    wide = groups * width
    hidden = active_ref.shape[1]
    heads = width // HEAD_DIM
    first_mid = groups * seqs
    last = first_mid + span // BLOCK - 1
    step = pl.program_id(0)
    me, at_plane = lax.axis_index("grp"), lax.axis_index("seq")
    side, pair = lax.rem(at_plane, 2), lax.div(at_plane, 2)
    group_device = [{"grp": xor(me, j, groups)} for j in range(groups)]
    pair_device = [{"seq": xor(at_plane, 2 * k, plane.size)} for k in range(plane.pairs)]
    partner = {"seq": xor(at_plane, 1, plane.size)}
    others = range(1, groups)

    def token_copy(j, s):
        owner = xor(me, j, groups)
        return remote(
            tok_ref.at[:, ds(owner * span + s * seq_len, seq_len, seq_len)],
            toks.at[j, :, ds(s * seq_len, seq_len, seq_len)],
            tok_send.at[j, s],
            tok_recv.at[j, s],
            group_device[j],
        )

    def cot_copy(j, s):
        start = xor(me, j, groups) * span + s * seq_len
        return remote(
            cot_ref.at[:, ds(start, seq_len, seq_len)],
            cots_out.at[j, :, ds(s * seq_len, seq_len, seq_len)],
            cot_send.at[j, s],
            cot_recv.at[j, s],
            group_device[j],
        )

    def vec_copy(j):
        source = vec_rows.at[2 if j == 3 else 0]
        device = group_device[1 if j == 3 else j]
        return remote(source, vec_rows.at[j], vec_send.at[j], vec_recv.at[j], device)

    q_rows = wq.shape[1] // plane.size

    def q_own(index, s):
        return ds((s * plane.pairs + index) * q_rows, q_rows, 16)

    def q1_copy(j):
        own = q_own(pair, side)
        source = wq.at[2 if j == 3 else 0, own, :]
        device = group_device[1 if j == 3 else j]
        return remote(source, wq.at[j, own, :], q1_send.at[j], q1_recv.at[j], device)

    q_groups = (pl.ds(1, 2), pl.ds(3, 1))

    def q2_copy(late, k, index):
        part = wq.at[q_groups[late], q_own(index, side), :]
        return remote(part, part, q2_send.at[late, k], q2_recv.at[late, k], pair_device[k])

    def q3_copy(late, s):
        rows = ds(s * plane.pairs * q_rows, plane.pairs * q_rows, 16)
        part = wq.at[q_groups[late], rows, :]
        return remote(part, part, q3_send.at[late], q3_recv.at[late], partner)

    half = rest.shape[2] // 2

    def rest_piece(index):
        down, along, size = plane.piece(index, half)
        return ds(down, plane.rows, 16), ds(side * half + along, size, 128)

    def r1_copy(j):
        down, along = rest_piece(pair)
        return remote(
            rest.at[2 if j == 3 else 0, down, along],
            rest.at[j, down, along],
            r1_send.at[j],
            r1_recv.at[j],
            group_device[1 if j == 3 else j],
        )

    def r2_copy(k, index):
        down, along = rest_piece(index)
        part = rest.at[pl.ds(1, groups - 1), down, along]
        return remote(part, part, r2_send.at[k], r2_recv.at[k], pair_device[k])

    def r3_copy(s):
        part = rest.at[pl.ds(1, groups - 1), :, ds(s * half, half, 128)]
        return remote(part, part, r3_send.at[0], r3_recv.at[0], partner)

    mine = ds(me * span, span, span)
    columns = [(0, wide), (wide, hidden), (wide + hidden, hidden)]
    local_copies = [
        (tok_ref.at[:, mine], toks.at[0]),
    ]
    local_copies += [
        (ref, rest.at[0, :, pl.ds(*place)]) for ref, place in zip(rest_refs, columns)
    ]
    local_copies += [
        (toks, toks_out),
        (wq.at[:, pl.ds(0, 3 * width), :], wq_out),
        (rest.at[:, :, pl.ds(wide, hidden)], inter_out),
        (vecs, vecs_out),
        (back_t, back_t_out),
        (out_t, out_t_out),
        (placed, placed_out),
    ]
    small = [(qkv_any[i], qkv_refs.at[i]) for i in range(3)]
    small += list(zip(vector_any, vector_refs))
    local_copies += small
    saves = [
        (result_ref, result_out),
        (mid_low_ref, mid_low_out),
        (normed1_ref, normed1_out),
        (normed2_ref, normed2_out),
        (active_ref, active_out),
        (slope_ref, slope_out),
    ]

    def save(i, b):
        part = pl.ds(b * BLOCK, BLOCK)
        source, target = saves[i]
        return pltpu.make_async_copy(
            source.at[:, :, part], target.at[:, :, part], save_sem.at[i, b]
        )

    def local_copy(i):
        return pltpu.make_async_copy(*local_copies[i], local_sem.at[i])

    @pl.when(step == 0)
    def _():
        greet(group_device[1:] + pair_device[1:] + [partner])
        smalls = range(len(local_copies) - len(small), len(local_copies))
        for i in (*smalls, 0, 1, 2, 3):
            local_copy(i).start()
        meet(group_device[1:] + pair_device[1:] + [partner])
        middle = (me == 1) | (me == 2)
        pl.when(middle)(lambda: token_copy(2, 0).start())
        pl.when(jnp.logical_not(middle))(lambda: token_copy(1, 0).start())
        vecs[...] = jnp.zeros_like(vecs)
        vec_rows[0] = jnp.zeros_like(vec_rows[0])
        for i in smalls:
            local_copy(i).wait()
        for i in range(VECTOR_COUNT - 1):
            vec_rows[0, i : i + 1, 0:width] = vector_refs[i][...]
        b_inter = jnp.concatenate([vector_refs[-1][i : i + 1] for i in range(hidden // 128)], axis=1)
        for a in range(hidden // width):
            i = B_INTER + a
            vec_rows[0, i : i + 1, 0:width] = b_inter[:, a * width : (a + 1) * width]
        for i in range(3):
            wq[0, i * width : (i + 1) * width, :] = qkv_refs[i].T
        if wq.shape[1] > 3 * width:
            wq[0, 3 * width :, :] = jnp.zeros_like(wq[0, 3 * width :, :])

        def start_small(j):
            q1_copy(j).start()
            vec_copy(j).start()

        @pl.when(middle)
        def _():
            start_small(1)
            start_small(2)

        @pl.when(jnp.logical_not(middle))
        def _():
            start_small(2)
            start_small(1)

        for i in (1, 2, 3):
            local_copy(i).wait()

        @pl.when(middle)
        def _():
            r1_copy(1).start()
            r1_copy(2).start()
            for j, s in ((2, 1), (1, 0), (1, 1)):
                token_copy(j, s).start()

        @pl.when(jnp.logical_not(middle))
        def _():
            r1_copy(2).start()
            r1_copy(1).start()
            for j, s in ((1, 1), (2, 0), (2, 1)):
                token_copy(j, s).start()

        local_copy(0).wait()
        vecs[0, :, 0:VECTORS] = vec_rows[0, :, 0:width].T

    @pl.when(step == 1)
    def _():
        for j in (1, 2):
            q1_copy(j).wait_recv()
            vec_copy(j).wait_recv()
        in_plane(side, plane.pairs, lambda k: q2_copy(0, k, pair).start())
        q1_copy(3).start()
        vec_copy(3).start()
        for j in (1, 2):
            vecs[j, :, 0:VECTORS] = vec_rows[j, :, 0:width].T

    @pl.when(step == seqs)
    def _():
        for k in range(1, plane.pairs):
            q2_copy(0, k, xor(pair, k, plane.pairs)).wait_recv()
        q3_copy(0, side).start()
        r1_copy(2).wait_recv()
        middle = (me == 1) | (me == 2)
        pl.when(jnp.logical_not(middle))(lambda: token_copy(3, 0).start())
        r1_copy(3).start()
        pl.when(middle)(lambda: token_copy(3, 0).start())
        for s in range(1, seqs):
            token_copy(3, s).start()
        q3_copy(0, 1 - side).wait_recv()

    for j in others:
        for s in range(seqs):

            @pl.when(step == j * seqs + s)
            def _():
                token_copy(j, s).wait_recv()

    @pl.when(step == 2 * seqs + 1)
    def _():
        for s in range(seqs):
            cot_copy(1, s).start()
        for s in range(seqs):
            for j in (2, 3):
                cot_copy(j, s).start()
        q1_copy(3).wait_recv()
        vec_copy(3).wait_recv()
        vecs[3, :, 0:VECTORS] = vec_rows[3, :, 0:width].T
        in_plane(side, plane.pairs, lambda k: q2_copy(1, k, pair).start())
        r1_copy(1).wait_recv()
        r1_copy(3).wait_recv()
        in_plane(side, plane.pairs, lambda k: r2_copy(k, pair).start())

    @pl.when(step == 3 * seqs)
    def _():
        for k in range(1, plane.pairs):
            q2_copy(1, k, xor(pair, k, plane.pairs)).wait_recv()
        q3_copy(1, side).start()
        q3_copy(1, 1 - side).wait_recv()

    @pl.when(step == 3 * seqs + 1)
    def _():
        for k in range(1, plane.pairs):
            r2_copy(k, xor(pair, k, plane.pairs)).wait_recv()
        r3_copy(side).start()

    @pl.when(step == first_mid)
    def _():
        r3_copy(1 - side).wait_recv()
        for i in () if fused else (4, 5, 6, 7, 10):
            local_copy(i).start()
        for g in range(groups):
            inter_t[g] = rest[g, :, wide : wide + hidden].T

    @pl.when(step == first_mid + 1)
    def _():
        for g in range(groups):
            back_t[g] = rest[g, :, wide + hidden : wide + 2 * hidden].T
            out_t[:, g * width : (g + 1) * width] = rest[g, :, 0:wide].T
        for i in () if fused else (8, 9):
            local_copy(i).start()

    @pl.when(step < first_mid)
    def _():
        j, s = lax.div(step, seqs), lax.rem(step, seqs)
        at = ds(s * seq_len, seq_len, seq_len)
        length = len_ref[me * seqs + s]
        drawn = mm(wq[j, 0 : 3 * width, :], toks[j, :, at])
        vec = vecs[j]
        qkv_ref[0, 0:width, :] = (
            (drawn[0:width] + vec[:, B_QUERY : B_QUERY + 1]) * (1.0 / math.sqrt(HEAD_DIM))
        ).astype(LOW)
        qkv_ref[0, width : 2 * width, :] = drawn[width : 2 * width].astype(LOW)
        qkv_ref[0, 2 * width :, :] = (
            drawn[2 * width :] + vec[:, B_VALUE : B_VALUE + 1]
        ).astype(LOW)
        row = lax.broadcasted_iota(jnp.int32, (16, seq_len), 0)
        place = lax.broadcasted_iota(jnp.int32, (16, seq_len), 1)
        mask_rows = jnp.where((row == 0) & (place >= length), MASKED, 0.0).astype(LOW)
        one_rows = jnp.where(row == 0, 1.0, 0.0).astype(LOW)
        inv_ref[...] = jnp.zeros_like(inv_ref)
        chunks = [(h, c) for h in range(heads) for c in range(0, seq_len, BLOCK)]

        def head(h):
            low, top = h * HEAD_DIM, (h + 1) * HEAD_DIM
            queries = jnp.concatenate([qkv_ref[0, low:top, :], one_rows], axis=0)
            keys = jnp.concatenate([qkv_ref[0, width + low : width + top, :], mask_rows], axis=0)
            values = jnp.concatenate(
                [qkv_ref[0, 2 * width + low : 2 * width + top, :], one_rows], axis=0
            )
            return queries, keys.T, values

        made = [head(0)]

        def scores_of(h, c):
            if h == len(made):
                made.append(head(h))
            queries, keys, _ = made[h]
            return mm(keys, queries[:, c : c + BLOCK])

        ready = scores_of(*chunks[0])
        for i, (h, c) in enumerate(chunks):
            scores = ready
            if i + 1 < len(chunks):
                ready = scores_of(*chunks[i + 1])
            low, top = h * HEAD_DIM, (h + 1) * HEAD_DIM
            best = jnp.max(scores, axis=0, keepdims=True)
            expo = jnp.exp(scores - best).astype(LOW)
            expo_ref[0, h, :, c : c + BLOCK] = expo
            context = mm(made[h][2], expo)
            inv = 1.0 / context[HEAD_DIM : HEAD_DIM + 1]
            inv_ref[0, h : h + 1, c : c + BLOCK] = inv
            ctx_ref[0, low:top, c : c + BLOCK] = (context[0:HEAD_DIM] * inv).astype(LOW)
        placed[ds(xor(me, j, groups) * width, width, width), at] = ctx_ref[0]

    @pl.when((step >= first_mid) & (step <= last))
    def _():
        at = ds((step - first_mid) * BLOCK, BLOCK, BLOCK)

        def column(group, which):
            return vecs[group, :, which : which + 1]

        context = placed[:, at]
        total = jnp.zeros((1, BLOCK), F32)
        for j in range(groups):
            rows = toks[j, :, at].astype(F32) + (
                mm(rest[j, :, 0:wide], context) + column(j, B_OUT)
            )
            total += jnp.sum(rows, axis=0, keepdims=True)
            resid[j] = rows
        mean = total * (1.0 / wide)
        total = jnp.zeros((1, BLOCK), F32)
        for j in range(groups):
            rows = resid[j] - mean
            total += jnp.sum(rows * rows, axis=0, keepdims=True)
        inv1 = lax.rsqrt(total * (1.0 / wide) + EPS)
        for j in range(groups):
            normed = (resid[j] - mean) * inv1
            normed1_ref[j, :, at] = normed.astype(LOW)
            rows = normed * column(j, GAIN1) + column(j, SHIFT1)
            resid[j] = rows
            mid_low_ref[j, :, at] = rows.astype(LOW)
        total = jnp.zeros((1, BLOCK), F32)
        for j in range(groups):
            for a in range(0, hidden, width):
                inner = mm(inter_t[j, a : a + width, :], mid_low_ref[j, :, at]) + column(
                    j, B_INTER + a // width
                )
                active, slope = gelu_parts(inner)
                active_ref[j, a : a + width, at] = active.astype(LOW)
                slope_ref[j, a : a + width, at] = slope.astype(LOW)
            rows = resid[j] + (
                mm(rest[j, :, wide + hidden : wide + 2 * hidden], active_ref[j, :, at])
                + column(j, B_BACK)
            )
            total += jnp.sum(rows, axis=0, keepdims=True)
            resid[j] = rows
        mean = total * (1.0 / wide)
        total = jnp.zeros((1, BLOCK), F32)
        for j in range(groups):
            rows = resid[j] - mean
            total += jnp.sum(rows * rows, axis=0, keepdims=True)
        inv2 = lax.rsqrt(total * (1.0 / wide) + EPS)
        for j in range(groups):
            normed = (resid[j] - mean) * inv2
            normed2_ref[j, :, at] = normed.astype(LOW)
            result_ref[j, :, at] = (normed * column(j, GAIN2) + column(j, SHIFT2)).astype(LOW)
        invs_ref[...] = jnp.zeros_like(invs_ref)
        invs_ref[0:1, :] = inv1
        invs_ref[1:2, :] = inv2

    for b in range(span // BLOCK):

        @pl.when(step == first_mid + b)
        def _():
            for i in range(1 if fused else len(saves)):
                save(i, b).start()

    def all_sent():
        for j in others:
            q1_copy(j).wait_send()
            vec_copy(j).wait_send()
            r1_copy(j).wait_send()
            for s in range(seqs):
                token_copy(j, s).wait_send()
                cot_copy(j, s).wait_send()
        for k in range(1, plane.pairs):
            for late in (0, 1):
                q2_copy(late, k, pair).wait_send()
            r2_copy(k, pair).wait_send()
        for late in (0, 1):
            q3_copy(late, side).wait_send()
        r3_copy(side).wait_send()

    def cots_here(s):
        for j in others:
            cot_copy(j, s).wait_recv()

    def all_saved():
        for i in range(1 if fused else len(saves)):
            for b in range(span // BLOCK):
                save(i, b).wait()

    if fused:
        return cots_here, all_saved, all_sent

    @pl.when(step == last)
    def _():
        all_sent()
        for s in range(seqs):
            cots_here(s)
        all_saved()
        for i in (4, 5, 6, 7, 8, 9, 10):
            local_copy(i).wait()


def forward(sizes, lengths, tokens, cotangent, weights, vectors):
    groups, plane, seq_len, hidden = sizes
    width, total = tokens.shape
    span = total // groups
    seqs, heads, wide = span // seq_len, width // HEAD_DIM, groups * width
    attention = groups * seqs
    steps = attention + span // BLOCK
    anywhere = pl.BlockSpec(memory_space=pl.ANY)
    wq_rows = round_up(3 * width, 16 * plane.size)
    rest_columns = plane.padded(wide + 2 * hidden)

    def group_at(t):
        return lax.div(jnp.minimum(t, attention - 1), seqs)

    def seq_at(t):
        return lax.rem(jnp.minimum(t, attention - 1), seqs)

    def block_at(t):
        return jnp.maximum(t - attention, 0)

    def by_seq(rows):
        return pl.BlockSpec((1, rows, seq_len), lambda t: (group_at(t), 0, seq_at(t)))

    def low(*shape):
        return jax.ShapeDtypeStruct(shape, LOW)

    dma = pltpu.SemaphoreType.DMA
    gate = [dma((groups,)), dma((groups,))]
    gather = gate + [dma((plane.pairs,)), dma((plane.pairs,)), dma((1,)), dma((1,))]
    gather_q = gate + [dma((2, plane.pairs)), dma((2, plane.pairs)), dma((2,)), dma((2,))]
    return pl.pallas_call(
        functools.partial(forward_kernel, groups, plane, seq_len),
        grid=(steps,),
        in_specs=[pl.BlockSpec(memory_space=pltpu.SMEM)]
        + [anywhere] * (8 + VECTOR_COUNT),
        out_specs=[anywhere] * 14
        + [
            by_seq(3 * width),
            pl.BlockSpec(
                (1, heads, seq_len, seq_len),
                lambda t: (jnp.minimum(t, attention - 1), 0, 0, 0),
            ),
            by_seq(8),
            by_seq(width),
            pl.BlockSpec((8, BLOCK), lambda t: (0, block_at(t))),
        ],
        out_shape=[
            low(groups, width, span),
            low(groups, width, span),
            low(groups, 3 * width, width),
            low(groups, width, hidden),
            low(groups, hidden, width),
            low(wide, wide),
            jax.ShapeDtypeStruct((groups, width, 128), F32),
            low(wide, span),
            low(groups, width, span),
            low(groups, width, span),
            low(groups, width, span),
            low(groups, width, span),
            low(groups, hidden, span),
            low(groups, hidden, span),
            low(groups, 3 * width, span),
            low(attention, heads, seq_len, seq_len),
            jax.ShapeDtypeStruct((groups, 8, span), F32),
            low(groups, width, span),
            jax.ShapeDtypeStruct((8, span), F32),
        ],
        scratch_shapes=[
            pltpu.VMEM((groups, width, span), LOW),
            pltpu.VMEM((groups, width, span), LOW),
            pltpu.VMEM((groups, width, span), LOW),
            pltpu.VMEM((groups, width, span), LOW),
            pltpu.VMEM((groups, hidden, span), LOW),
            pltpu.VMEM((groups, hidden, span), LOW),
            dma((6, span // BLOCK)),
            pltpu.VMEM((groups, width, span), LOW),
            pltpu.VMEM((groups, wq_rows, width), LOW),
            pltpu.VMEM((groups, width, rest_columns), LOW),
            pltpu.VMEM((groups, VECTORS, round_up(width, 128)), F32),
            pltpu.VMEM((groups, width, 128), F32),
            pltpu.VMEM((wide, span), LOW),
            pltpu.VMEM((groups, hidden, width), LOW),
            pltpu.VMEM((groups, hidden, width), LOW),
            pltpu.VMEM((wide, wide), LOW),
            pltpu.VMEM((groups, width, BLOCK), F32),
            pltpu.VMEM((3, width, width), LOW),
        ]
        + [pltpu.VMEM(vector.shape, F32) for vector in vectors]
        + [
            dma((14 + VECTOR_COUNT,)),
            dma((groups, seqs)),
            dma((groups, seqs)),
        ]
        + [dma((groups, seqs)), dma((groups, seqs))]
        + gate
        + gather_q
        + gather,
        compiler_params=pltpu.CompilerParams(
            vmem_limit_bytes=VMEM_BYTES, collective_id=0, has_side_effects=True
        ),
        name="forward",
    )(lengths, tokens, cotangent, *weights, *vectors)


def lanes(block):
    folded = block[:, 0:128]
    for c in range(128, block.shape[1], 128):
        folded = folded + block[:, c : c + 128]
    return folded


def backward_kernel(
    groups,
    plane,
    seq_len,
    result_ref,
    cot_any,
    cots_any,
    placed_any,
    mid_low_any,
    normed1_any,
    normed2_any,
    invs_any,
    active_any,
    slope_any,
    qkv_any,
    expo_any,
    inv_any,
    ctx_any,
    toks_any,
    wq_any,
    inter_any,
    back_t_any,
    out_t_any,
    vecs_any,
    result_out,
    gtok_out,
    grest_out,
    gqkv_out,
    vecs_ref,
    invs_ref,
    back_t,
    inter_ref,
    out_t,
    cots_ref,
    normed1_ref,
    normed2_ref,
    qkv_ref,
    expo_ref,
    inv_ref,
    ctx_ref,
    toks_ref,
    seq_sem,
    wq_ref,
    placed_ref,
    mid_low_ref,
    active_ref,
    load_sem,
    grads,
    ffn,
    branch,
    inner,
    sums,
    stack,
    acc,
    acc_q,
    pair_got,
    plane_got,
    group_sent,
    group_got,
    total_rest,
    pair_sent_q,
    pair_got_q,
    plane_got_q,
    group_sent_q,
    group_got_q,
    total_q,
    local_sem,
    result_send,
    result_recv,
    gtok_send,
    gtok_recv,
    pair_send,
    pair_recv,
    plane_send,
    plane_recv,
    group_send,
    group_recv,
    spread_send,
    spread_recv,
    join_send,
    join_recv,
    fused_from=None,
    arrived=None,
):
    fused = fused_from is not None
    gctx = cots_ref
    width, span = gctx.shape[1:]
    seqs = span // seq_len
    wide = groups * width
    hidden = inner.shape[1]
    heads = width // HEAD_DIM
    blocks = span // BLOCK
    last = blocks + groups * seqs - 1
    step = pl.program_id(0) - (fused_from or 0)
    me, at_plane = lax.axis_index("grp"), lax.axis_index("seq")
    side, pair = lax.rem(at_plane, 2), lax.div(at_plane, 2)
    group_device = [{"grp": xor(me, j, groups)} for j in range(groups)]
    pair_device = [{"seq": xor(at_plane, 2 * k, plane.size)} for k in range(plane.pairs)]
    partner = {"seq": xor(at_plane, 1, plane.size)}
    others, mates = range(1, groups), range(1, plane.pairs)

    seq_loads = (0, 1) if fused else range(4)
    loads = [] if fused else [
        (vecs_any, vecs_ref),
        (invs_any, invs_ref),
        (back_t_any, back_t),
        (inter_any, inter_ref),
        (out_t_any, out_t),
        (wq_any, wq_ref),
        (inv_any, inv_ref),
        (placed_any, placed_ref),
        (mid_low_any, mid_low_ref),
        (active_any, active_ref),
    ]

    def load(i):
        return pltpu.make_async_copy(*loads[i], load_sem.at[i])

    away = pl.ds(1, groups - 1)
    block_loads = [] if fused else [
        (cots_any.at[away], cots_ref.at[away]),
        (normed2_any, normed2_ref),
        (slope_any, inner),
        (normed1_any, normed1_ref),
        (cot_any, cots_ref.at[0]),
    ]

    def load_block(i, b):
        part = pl.ds(b * BLOCK, BLOCK)
        source, target = block_loads[i]
        sem = load_sem.at[len(loads) + i * blocks + b]
        if i == 4:
            own = ds(me * span + b * BLOCK, BLOCK, BLOCK)
            return pltpu.make_async_copy(source.at[:, own], target.at[:, part], sem)
        return pltpu.make_async_copy(source.at[:, :, part], target.at[:, :, part], sem)

    def load_seq(i, order):
        j, s, slot = groups - 1 - order // seqs, order % seqs, order % 2
        part = pl.ds(s * seq_len, seq_len)
        source, target = (
            (qkv_any.at[j, :, part], qkv_ref),
            (expo_any.at[j * seqs + s], expo_ref),
            (ctx_any.at[j, :, part], ctx_ref),
            (toks_any.at[j, :, part], toks_ref),
        )[i]
        return pltpu.make_async_copy(source, target.at[slot], seq_sem.at[i, order])

    def result_copy(j):
        mine = result_out.at[:, ds(me * span, span, span)]
        return remote(
            result_ref.at[j], mine, result_send.at[j], result_recv.at[j], group_device[j]
        )

    def result_landing(j):
        there = result_out.at[:, ds(xor(me, j, groups) * span, span, span)]
        return remote(there, there, result_send.at[j], result_recv.at[j], group_device[j])

    def gtok_copy(j, s):
        mine = gtok_out.at[:, ds(me * span + s * seq_len, seq_len, seq_len)]
        block = gctx.at[j, :, ds(s * seq_len, seq_len, seq_len)]
        if j == 0:
            return pltpu.make_async_copy(block, mine, local_sem.at[1 + s])
        return remote(block, mine, gtok_send.at[j, s], gtok_recv.at[j, s], group_device[j])

    def gtok_landing(j, s):
        start = xor(me, j, groups) * span + s * seq_len
        there = gtok_out.at[:, ds(start, seq_len, seq_len)]
        return remote(there, there, gtok_send.at[j, s], gtok_recv.at[j, s], group_device[j])

    def buffers(number):
        if number == 0:
            return (
                acc,
                acc,
                pair_got,
                plane_got,
                group_sent,
                group_got,
                total_rest,
                pl.ds(0, groups),
            )
        return (
            acc_q,
            pair_sent_q,
            pair_got_q,
            plane_got_q,
            group_sent_q,
            group_got_q,
            total_q,
            pl.ds(number - 1, 1),
        )

    def pair_copy(number):
        full, sent, got, *_, lead = buffers(number)
        half = full.shape[2] // 2
        there = ds((1 - side) * half, half, 128) if number == 0 else pl.ds(0, half)
        return remote(
            sent.at[lead, :, there],
            got.at[lead, :, pl.ds(0, half)],
            pair_send.at[number],
            pair_recv.at[number],
            partner,
        )

    def piece_of(ref, index):
        down, along, size = plane.piece(index, ref.shape[2])
        return ds(down, plane.rows, 16), ds(along, size, 128)

    def plane_copy(number, k):
        _, _, sent, got, *_, lead = buffers(number)
        down, along = piece_of(sent, xor(pair, k, plane.pairs))
        return remote(
            sent.at[lead, down, along],
            got.at[k, lead],
            plane_send.at[number, k],
            plane_recv.at[number, k],
            pair_device[k],
        )

    def group_copy(number, j):
        sent, got = buffers(number)[4:6]
        return remote(
            sent.at[j],
            got.at[j],
            group_send.at[number, j],
            group_recv.at[number, j],
            group_device[1 if j == 3 else j],
        )

    def total_piece(total, index):
        half = total.shape[1] // 2
        down, along, size = plane.piece(index, half)
        return total.at[ds(down, plane.rows, 16), ds(side * half + along, size, 128)]

    def spread_copy(number, k, index):
        part = total_piece(buffers(number)[6], index)
        return remote(
            part, part, spread_send.at[number, k], spread_recv.at[number, k], pair_device[k]
        )

    def join_copy(number, s):
        total = buffers(number)[6]
        half = total.shape[1] // 2
        part = total.at[:, ds(s * half, half, 128)]
        return remote(part, part, join_send.at[number], join_recv.at[number], partner)

    def start_pair(number):
        full, sent, *_, lead = buffers(number)
        half = full.shape[2] // 2
        if number:
            sent[lead, :, 0:half] = full[lead, :, ds((1 - side) * half, half, 128)].astype(LOW)
        pair_copy(number).start()

    def start_plane(number):
        full, _, got, *_, lead = buffers(number)
        half = full.shape[2] // 2
        pair_copy(number).wait_recv()
        summed = full[lead, :, ds(side * half, half, 128)].astype(F32)
        summed = summed + got[lead, :, 0:half].astype(F32)
        got[lead, :, 0:half] = summed.astype(LOW)
        in_plane(side, plane.pairs, lambda k: plane_copy(number, k).start())

    def plane_sum(number):
        _, _, held, got, *_, lead = buffers(number)
        for k in mates:
            plane_copy(number, k).wait_recv()
        down, along = piece_of(held, pair)
        summed = held[lead, down, along].astype(F32)
        for k in mates:
            summed = summed + got[k, lead].astype(F32)
        return summed

    def start_group(number):
        summed = plane_sum(number)
        sent, got = buffers(number)[4:6]
        if number == 0:
            for j in range(groups):
                sent[j] = summed[j].astype(LOW)
            group_copy(0, 3).start()
            group_copy(0, 1).start()
            return
        j, summed = number - 1, summed[0]
        if j == 2:
            group_copy(1, 3).wait_recv()
            summed = summed + got[3].astype(F32)
        sent[j] = summed.astype(LOW)
        group_copy(1, j).start()

    def hand_on():
        group_copy(0, 3).wait_recv()
        group_sent[2] = (group_sent[2].astype(F32) + group_got[3].astype(F32)).astype(LOW)
        group_copy(0, 2).start()

    def start_spread(number, summed):
        got, total = buffers(number)[5:7]
        for j in (1, 2):
            group_copy(number, j).wait_recv()
            summed = summed + got[j].astype(F32)
        total_piece(total, pair)[...] = summed.astype(LOW)
        in_plane(side, plane.pairs, lambda k: spread_copy(number, k, pair).start())

    def start_join(number):
        for k in mates:
            spread_copy(number, k, xor(pair, k, plane.pairs)).wait_recv()
        join_copy(number, side).start()

    @pl.when(step == 0)
    def _():
        if not fused:
            greet(group_device[1:] + pair_device[1:] + [partner])
            for i in range(3):
                load(i).start()
            for i in range(len(block_loads)):
                load_block(i, 0).start()
            for i in (3, 4):
                load(i).start()
            meet(group_device[1:] + pair_device[1:] + [partner])
        in_turn(me, lambda j: result_copy(j).start())
        for b in range(1, blocks):
            for i in range(len(block_loads)):
                load_block(i, b).start()
        for i in range(0 if fused else 5, len(loads)):
            load(i).start()
        for i in seq_loads:
            load_seq(i, 0).start()
        for ref in (acc_q, sums):
            ref[...] = jnp.zeros_like(ref)
        for i in () if fused else range(5):
            load(i).wait()

    for b in range(blocks):

        @pl.when(step == b)
        def _():
            for i in range(len(block_loads)):
                load_block(i, b).wait()
            if fused:
                arrived(b)

    for order in range(groups * seqs):

        @pl.when(step == blocks + order)
        def _():
            for i in seq_loads:
                load_seq(i, order).wait()
                if order + 1 < groups * seqs:
                    load_seq(i, order + 1).start()

    @pl.when((step >= 0) & (step < blocks))
    def _():
        at = ds(step * BLOCK, BLOCK, BLOCK)

        def column(group, which):
            return vecs_ref[group, :, which : which + 1]

        inv1, inv2 = invs_ref[0:1, at], invs_ref[1:2, at]
        zero = jnp.zeros((1, BLOCK), F32)
        first, second = zero, zero
        for j in range(groups):
            rows = cots_ref[j, :, at].astype(F32)
            normed = normed2_ref[j, :, at].astype(F32)
            scaled = rows * column(j, GAIN2)
            first += jnp.sum(scaled, axis=0, keepdims=True)
            second += jnp.sum(scaled * normed, axis=0, keepdims=True)
            sums[GAIN2 - B_OUT, j] += lanes(rows * normed)
            sums[SHIFT2 - B_OUT, j] += lanes(rows)
        first, second = first * (1.0 / wide), second * (1.0 / wide)
        next_first, next_second = zero, zero
        for j in range(groups):
            scaled = cots_ref[j, :, at].astype(F32) * column(j, GAIN2)
            rows = inv2 * (scaled - first - normed2_ref[j, :, at].astype(F32) * second)
            low_rows = rows.astype(LOW)
            sums[B_BACK - B_OUT, j] += lanes(low_rows.astype(F32))
            ffn[j, :, at] = low_rows
            for a in range(0, hidden, width):
                inner[j, a : a + width, at] = (
                    mm(back_t[j, a : a + width, :], low_rows).astype(LOW)
                    * inner[j, a : a + width, at]
                )
            rows = rows + mm(inter_ref[j], inner[j, :, at])
            normed = normed1_ref[j, :, at].astype(F32)
            sums[GAIN1 - B_OUT, j] += lanes(rows * normed)
            sums[SHIFT1 - B_OUT, j] += lanes(rows)
            scaled = rows * column(j, GAIN1)
            next_first += jnp.sum(scaled, axis=0, keepdims=True)
            next_second += jnp.sum(scaled * normed, axis=0, keepdims=True)
            grads[j] = scaled
        first, second = next_first * (1.0 / wide), next_second * (1.0 / wide)
        for j in range(groups):
            rows = inv1 * (grads[j] - first - normed1_ref[j, :, at].astype(F32) * second)
            low_rows = rows.astype(LOW)
            branch[j * width : (j + 1) * width, at] = low_rows
            sums[0, j] += lanes(low_rows.astype(F32))
        for j in range(groups):
            there = ds(xor(me, j, groups) * width, width, width)
            gctx[j, :, at] = mm(out_t[there, :], branch[:, at]).astype(LOW)

    @pl.when(step == blocks - 1)
    def _():
        for i in range(0 if fused else 5, len(loads)):
            load(i).wait()
        lane = lax.broadcasted_iota(jnp.int32, (width, 128), 1)
        ones = jnp.ones((16, span), LOW)
        for j in range(groups):
            rows = slice(j * width, (j + 1) * width)
            acc[j, :, 0:wide] = mm_nt(branch[rows, :], placed_ref[...]).astype(LOW)
            both = mm_nt(jnp.concatenate([mid_low_ref[j], ones], axis=0), inner[j])
            acc[j, :, wide : wide + hidden] = both[0:width].astype(LOW)
            acc[j, :, wide + hidden : wide + 2 * hidden] = mm_nt(ffn[j], active_ref[j]).astype(LOW)
            small = jnp.zeros((width, 128), F32)
            for which in (B_OUT, GAIN1, SHIFT1, B_BACK, GAIN2, SHIFT2):
                added = jnp.sum(sums[which - B_OUT, j], axis=1, keepdims=True)
                small = jnp.where(lane == which, added, small)
            for a in range(0, hidden, width):
                added = both[width : width + 8, a : a + width].T[:, 0:1]
                small = jnp.where(lane == B_INTER + a // width, added, small)
            acc[j, :, wide + 2 * hidden : wide + 2 * hidden + 128] = small.astype(LOW)
        if acc.shape[2] > wide + 2 * hidden + 128:
            acc[:, :, wide + 2 * hidden + 128 :] = jnp.zeros_like(acc[:, :, wide + 2 * hidden + 128 :])
        start_pair(0)

    @pl.when(step >= blocks)
    def _():
        order = step - blocks
        j, s, slot = groups - 1 - lax.div(order, seqs), lax.rem(order, seqs), lax.rem(order, 2)
        at = ds(s * seq_len, seq_len, seq_len)
        row = lax.broadcasted_iota(jnp.int32, (16, seq_len), 0)
        minus_rows = jnp.where(row < 3, -1.0, 0.0).astype(LOW)
        chunks = [(h, c) for h in range(heads) for c in range(0, seq_len, BLOCK)]

        def context_of(low, top):
            if fused:
                start = xor(me, j, groups) * width + low
                return placed_ref[ds(start, HEAD_DIM, HEAD_DIM), at]
            return ctx_ref[slot, low:top, :]

        def head(h):
            low, top = h * HEAD_DIM, (h + 1) * HEAD_DIM
            values = jnp.concatenate(
                [qkv_ref[slot, 2 * width + low : 2 * width + top, :], minus_rows], axis=0
            )
            scaled = (gctx[j, low:top, at].astype(F32) * inv_ref[j, h : h + 1, at]).astype(LOW)
            delta = jnp.sum(
                scaled.astype(F32) * context_of(low, top).astype(F32), axis=0, keepdims=True
            )
            first = delta.astype(LOW).astype(F32)
            second = (delta - first).astype(LOW).astype(F32)
            third = delta - first - second
            parts = jnp.where(
                row == 0, first, jnp.where(row == 1, second, jnp.where(row == 2, third, 0.0))
            ).astype(LOW)
            return values.T, scaled, jnp.concatenate([scaled, parts], axis=0)

        made = [head(0)]

        def shifted_of(h, c):
            if h == len(made):
                made.append(head(h))
            return mm(made[h][0], made[h][2][:, c : c + BLOCK])

        ready = shifted_of(*chunks[0])
        for i, (h, c) in enumerate(chunks):
            shifted = ready
            if i + 1 < len(chunks):
                ready = shifted_of(*chunks[i + 1])
            low, top = h * HEAD_DIM, (h + 1) * HEAD_DIM
            part = slice(c, c + BLOCK)
            expo = expo_ref[slot, h, :, part]
            grad_s = expo * shifted.astype(LOW)
            add_k = mm_nt(qkv_ref[slot, low:top, part], grad_s)
            add_v = mm_nt(made[h][1][:, part], expo)
            grad_k = add_k if c == 0 else grad_k + add_k
            grad_v = add_v if c == 0 else grad_v + add_v
            stack[low:top, part] = (
                mm(qkv_ref[slot, width + low : width + top, :], grad_s) * (1.0 / math.sqrt(HEAD_DIM))
            ).astype(LOW)
            if c + BLOCK == seq_len:
                stack[width + low : width + top, :] = grad_k.astype(LOW)
                stack[2 * width + low : 2 * width + top, :] = grad_v.astype(LOW)
        rows = stack[...]
        gctx[j, :, at] = (
            branch[ds(j * width, width, width), at].astype(F32) + mm_tn(wq_ref[j], rows)
        ).astype(LOW)
        acc_q[j, :, 0 : 3 * width] += mm_nt(toks_ref[j, :, at] if fused else toks_ref[slot], rows)
        added = jnp.sum(rows.astype(F32), axis=1, keepdims=True)
        lane = lax.broadcasted_iota(jnp.int32, (width, 128), 1)
        acc_q[j, :, 3 * width : 3 * width + 128] += jnp.where(
            lane == B_QUERY, added[0:width], jnp.where(lane == B_VALUE, added[2 * width :], 0.0)
        )

    middle = (me == 1) | (me == 2)

    def outer_sends(j, s):
        pl.when(jnp.logical_not(middle))(lambda: gtok_copy(j, s).start())

    def middle_sends(first, second):
        for core, pieces in ((0, first), (1, second)):

            @pl.when(middle & (side == core))
            def _():
                for j, s in pieces:
                    gtok_copy(j, s).start()

    def first_step():
        outer_sends(3, 0)
        start_plane(0)

    def second_step():
        outer_sends(3, 1)
        start_pair(4)

    def third_step():
        outer_sends(2, 0)
        start_plane(4)

    def fourth_step():
        outer_sends(2, 1)
        start_pair(3)

    def fifth_step():
        middle_sends([(3, 0)], [(3, 0)])
        start_plane(3)

    def sixth_step():
        start_group(0)
        middle_sends([(1, 0)], [(3, 1)])
        start_pair(2)
        start_group(4)

    def seventh_step():
        hand_on()
        start_plane(2)
        start_group(3)
        outer_sends(1, 0)
        outer_sends(1, 1)
        middle_sends([(1, 1)], [(2, 0)])
        gtok_copy(0, 0).start()

    def eighth_step():
        start_pair(1)
        start_group(2)
        middle_sends([(3, 1), (2, 0), (2, 1)], [(2, 1), (1, 0), (1, 1)])
        gtok_copy(0, 1).start()

    for order, finish_step in enumerate(
        (
            first_step,
            second_step,
            third_step,
            fourth_step,
            fifth_step,
            sixth_step,
            seventh_step,
            eighth_step,
        )
    ):
        pl.when(step == blocks + order)(finish_step)

    @pl.when(step == last)
    def _():
        start_plane(1)
        start_spread(0, group_sent[0].astype(F32))
        start_spread(1, plane_sum(1)[0])
        start_join(0)
        start_join(1)
        join_copy(0, 1 - side).wait_recv()
        rest_done = pltpu.make_async_copy(total_rest, grest_out, local_sem.at[1 + seqs])
        rest_done.start()
        join_copy(1, 1 - side).wait_recv()
        q_done = pltpu.make_async_copy(total_q, gqkv_out, local_sem.at[2 + seqs])
        q_done.start()
        for s in range(seqs):
            gtok_copy(0, s).wait()
        for j in others:
            result_copy(j).wait_send()
            result_landing(j).wait_recv()
            for s in range(seqs):
                gtok_copy(j, s).wait_send()
                gtok_landing(j, s).wait_recv()
            for number in (0, 1):
                group_copy(number, j).wait_send()
        for number in range(1 + groups):
            pair_copy(number).wait_send()
            for k in mates:
                plane_copy(number, k).wait_send()
        for number in (0, 1):
            for k in mates:
                spread_copy(number, k, pair).wait_send()
            join_copy(number, side).wait_send()
        rest_done.wait()
        q_done.wait()


def sum_buffers(groups, width, plane, columns):
    half = columns // 2
    size = half // plane.col_parts
    return [
        pltpu.VMEM((groups, width, half), LOW),
        pltpu.VMEM((plane.pairs, groups, plane.rows, size), LOW),
        pltpu.VMEM((groups, plane.rows, size), LOW),
        pltpu.VMEM((groups, plane.rows, size), LOW),
        pltpu.VMEM((width, columns), LOW),
    ]


def sum_semaphores(groups, seqs, plane):
    dma = pltpu.SemaphoreType.DMA
    numbers = 1 + groups
    shapes = [(3 + seqs,)] + [(groups,)] * 2 + [(groups, seqs)] * 2 + [(numbers,)] * 2
    shapes += [(numbers, plane.pairs)] * 2 + [(2, groups)] * 2 + [(2, plane.pairs)] * 2 + [(2,)] * 2
    return [dma(shape) for shape in shapes]


def backward(sizes, cotangent, made):
    groups, plane, seq_len, hidden = sizes
    cots, toks, wq, inter, back_t, out_t, vecs, placed, result, mid_low, normed1, normed2 = made[0:12]
    active, slope, qkv, expo, inv, ctx, invs = made[12:]
    width, span = toks.shape[1:]
    seqs, heads, wide = span // seq_len, width // HEAD_DIM, groups * width
    blocks, attention = span // BLOCK, groups * seqs
    columns = plane.padded(wide + 2 * hidden + 128)
    columns_q = plane.padded(3 * width + 128)
    anywhere = pl.BlockSpec(memory_space=pl.ANY)

    def low(*shape):
        return jax.ShapeDtypeStruct(shape, LOW)

    dma = pltpu.SemaphoreType.DMA
    return pl.pallas_call(
        functools.partial(backward_kernel, groups, plane, seq_len),
        grid=(blocks + attention,),
        in_specs=[anywhere] * 20,
        out_specs=[anywhere] * 4,
        out_shape=[
            low(width, groups * span),
            low(width, groups * span),
            low(width, columns),
            low(width, columns_q),
        ],
        scratch_shapes=[
            pltpu.VMEM(vecs.shape, F32),
            pltpu.VMEM(invs.shape, F32),
            pltpu.VMEM(back_t.shape, LOW),
            pltpu.VMEM(inter.shape, LOW),
            pltpu.VMEM(out_t.shape, LOW),
            pltpu.VMEM(cots.shape, LOW),
            pltpu.VMEM(normed1.shape, LOW),
            pltpu.VMEM(normed2.shape, LOW),
            pltpu.VMEM((2, 3 * width, seq_len), LOW),
            pltpu.VMEM((2, heads, seq_len, seq_len), LOW),
            pltpu.VMEM(inv.shape, F32),
            pltpu.VMEM((2, width, seq_len), LOW),
            pltpu.VMEM((2, width, seq_len), LOW),
            dma((4, groups * seqs)),
            pltpu.VMEM(wq.shape, LOW),
            pltpu.VMEM(placed.shape, LOW),
            pltpu.VMEM(mid_low.shape, LOW),
            pltpu.VMEM(active.shape, LOW),
            dma((10 + 5 * blocks,)),
            pltpu.VMEM((groups, width, BLOCK), F32),
            pltpu.VMEM((groups, width, span), LOW),
            pltpu.VMEM((wide, span), LOW),
            pltpu.VMEM((groups, hidden, span), LOW),
            pltpu.VMEM((B_INTER - B_OUT, groups, width, 128), F32),
            pltpu.VMEM((3 * width, seq_len), LOW),
            pltpu.VMEM((groups, width, round_up(wide + 2 * hidden + 128, 256)), LOW),
            pltpu.VMEM((groups, width, round_up(3 * width + 128, 256)), F32),
        ]
        + sum_buffers(groups, width, plane, columns)
        + [pltpu.VMEM((groups, width, columns_q // 2), LOW)]
        + sum_buffers(groups, width, plane, columns_q)
        + sum_semaphores(groups, seqs, plane),
        compiler_params=pltpu.CompilerParams(
            vmem_limit_bytes=VMEM_BYTES, collective_id=1, has_side_effects=True
        ),
        name="backward",
    )(
        result,
        cotangent,
        cots,
        placed,
        mid_low,
        normed1,
        normed2,
        invs,
        active,
        slope,
        qkv,
        expo,
        inv,
        ctx,
        toks,
        wq,
        inter,
        back_t,
        out_t,
        vecs,
    )


def fused_kernel(groups, plane, seq_len, *refs):
    refs = list(refs)

    def take(count):
        taken = refs[0:count]
        del refs[0:count]
        return taken

    len_ref, tok_ref, cot_ref = take(3)
    rest_refs, qkv_any, vector_any = take(3), take(3), take(VECTOR_COUNT)
    result_any, qkv_hbm, expo_hbm, *outs = take(7)
    toks, wq, rest, vec_rows, vecs, placed, inter_t, back_t, out_t, resid, qkv_refs = take(11)
    vector_refs = take(VECTOR_COUNT)
    result, mid_low, normed1, normed2, active, slope, cots = take(7)
    qkv_slots, expo_slots, ctx_slot, inv_all, invs = take(5)
    save_sem, local_sem, store_sem, own_sem = take(4)
    forward_sems = take(18)
    width, span = toks.shape[1:]
    seqs, wide, hidden = span // seq_len, groups * width, active.shape[1]
    steps = groups * seqs
    offset = steps + span // BLOCK
    step = pl.program_id(0)
    me = lax.axis_index("grp")

    def stores(k):
        j, s, slot = k // seqs, k % seqs, k % 2
        there = qkv_hbm.at[j, :, pl.ds(s * seq_len, seq_len)]
        return [
            pltpu.make_async_copy(qkv_slots.at[slot], there, store_sem.at[0, k]),
            pltpu.make_async_copy(expo_slots.at[slot], expo_hbm.at[k], store_sem.at[1, k]),
        ]

    own_cot = pltpu.make_async_copy(
        cot_ref.at[:, ds(me * span, span, span)], cots.at[0], own_sem.at[0]
    )
    for k in range(steps):

        @pl.when(step == k + 2)
        def _():
            for copy in stores(k):
                copy.wait()

    at_step = jnp.minimum(step, steps - 1)
    j, s = lax.div(at_step, seqs), lax.rem(at_step, seqs)
    slot = pl.ds(lax.rem(at_step, 2), 1)
    block = jnp.minimum(jnp.maximum(step - steps, 0), span // BLOCK - 1)
    cots_here, all_saved, all_sent = forward_steps(
        groups,
        plane,
        seq_len,
        len_ref,
        tok_ref,
        cot_ref,
        rest_refs,
        qkv_any,
        vector_any,
        (cots,) + (None,) * 7,
        (result_any,) + (None,) * 5,
        (
            qkv_slots.at[slot],
            expo_slots.at[slot],
            inv_all.at[pl.ds(j, 1), :, ds(s * seq_len, seq_len, seq_len)],
            ctx_slot,
            invs.at[:, ds(block * BLOCK, BLOCK, BLOCK)],
        ),
        (result, mid_low, normed1, normed2, active, slope, save_sem),
        (toks, wq, rest, vec_rows, vecs, placed, inter_t, back_t, out_t, resid),
        qkv_refs,
        vector_refs,
        local_sem,
        *forward_sems,
        fused=True,
    )
    for k in range(steps):

        @pl.when(step == k)
        def _():
            for copy in stores(k):
                copy.start()

    pl.when(step == 1)(own_cot.start)

    pl.when(step == offset)(all_saved)

    def arrived(b):
        per_seq = seq_len // BLOCK
        if b == 0:
            own_cot.wait()
        if b % per_seq == 0:
            cots_here(b // per_seq)

    backward_kernel(
        groups,
        plane,
        seq_len,
        result_any,
        *(None,) * 9,
        qkv_hbm,
        expo_hbm,
        None,
        qkv_hbm,
        qkv_hbm,
        *(None,) * 5,
        *outs,
        vecs,
        invs,
        back_t,
        rest.at[:, :, pl.ds(wide, hidden)],
        out_t,
        cots,
        normed1,
        normed2,
        qkv_slots,
        expo_slots,
        inv_all,
        ctx_slot,
        toks,
        take(1)[0],
        wq.at[:, pl.ds(0, 3 * width), :],
        placed,
        mid_low,
        active,
        None,
        resid,
        result,
        take(1)[0],
        slope,
        *refs,
        fused_from=offset,
        arrived=arrived,
    )
    pl.when(step == offset + span // BLOCK + steps - 1)(all_sent)


def fused(sizes, lengths, tokens, cotangent, weights, vectors):
    groups, plane, seq_len, hidden = sizes
    width, total = tokens.shape
    span = total // groups
    seqs, heads, wide = span // seq_len, width // HEAD_DIM, groups * width
    attention, blocks = groups * seqs, span // BLOCK
    wq_rows = round_up(3 * width, 16 * plane.size)
    rest_columns = plane.padded(wide + 2 * hidden)
    columns = plane.padded(wide + 2 * hidden + 128)
    columns_q = plane.padded(3 * width + 128)
    anywhere = pl.BlockSpec(memory_space=pl.ANY)
    dma = pltpu.SemaphoreType.DMA

    def low(*shape):
        return jax.ShapeDtypeStruct(shape, LOW)

    def keep(*shape):
        return pltpu.VMEM(shape, LOW)

    def keep_f32(*shape):
        return pltpu.VMEM(shape, F32)

    gate = [dma((groups,)), dma((groups,))]
    by_token, by_hidden = keep(groups, width, span), keep(groups, hidden, span)
    forward_scratch = [
        by_token,
        keep(groups, wq_rows, width),
        keep(groups, width, rest_columns),
        keep_f32(groups, VECTORS, round_up(width, 128)),
        keep_f32(groups, width, 128),
        keep(wide, span),
        keep(groups, hidden, width),
        keep(groups, hidden, width),
        keep(wide, wide),
        keep_f32(groups, width, BLOCK),
        keep(3, width, width),
    ]
    forward_scratch += [keep_f32(*vector.shape) for vector in vectors]
    forward_scratch += [by_token] * 4 + [by_hidden] * 2 + [by_token]
    forward_scratch += [
        keep(2, 3 * width, seq_len),
        keep(2, heads, seq_len, seq_len),
        keep(1, width, seq_len),
        keep_f32(groups, 8, span),
        keep_f32(8, span),
        dma((6, blocks)),
        dma((14 + VECTOR_COUNT,)),
        dma((2, attention)),
        dma((1,)),
    ]
    forward_scratch += [dma((groups, seqs))] * 4 + gate
    forward_scratch += gate + [dma((2, plane.pairs)), dma((2, plane.pairs)), dma((2,)), dma((2,))]
    forward_scratch += gate + [dma((plane.pairs,)), dma((plane.pairs,)), dma((1,)), dma((1,))]
    backward_scratch = [
        dma((4, attention)),
        keep(wide, span),
        keep_f32(B_INTER - B_OUT, groups, width, 128),
        keep(3 * width, seq_len),
        keep(groups, width, round_up(wide + 2 * hidden + 128, 256)),
        keep_f32(groups, width, round_up(3 * width + 128, 256)),
    ]
    backward_scratch += sum_buffers(groups, width, plane, columns)
    backward_scratch += [keep(groups, width, columns_q // 2)]
    backward_scratch += sum_buffers(groups, width, plane, columns_q)
    backward_scratch += sum_semaphores(groups, seqs, plane)
    return pl.pallas_call(
        functools.partial(fused_kernel, groups, plane, seq_len),
        grid=(2 * (attention + blocks),),
        in_specs=[pl.BlockSpec(memory_space=pltpu.SMEM)] + [anywhere] * (8 + VECTOR_COUNT),
        out_specs=[anywhere] * 7,
        out_shape=[
            low(groups, width, span),
            low(groups, 3 * width, span),
            low(attention, heads, seq_len, seq_len),
            low(width, total),
            low(width, total),
            low(width, columns),
            low(width, columns_q),
        ],
        scratch_shapes=forward_scratch + backward_scratch,
        compiler_params=pltpu.CompilerParams(
            vmem_limit_bytes=VMEM_BYTES, collective_id=2, has_side_effects=True
        ),
        name="layer",
    )(lengths, tokens, cotangent, *weights, *vectors)


FINISH_PARTS = 4


def finish_kernel(groups, hidden, own_ref, result_ref, gtok_ref, rest_ref, qkv_ref, *refs):
    outs, refs = refs[0:17], refs[17:]
    result, gtok_low, gtok, rest, qkv, *made, in_sem, out_sem = refs
    width, rows = result_ref.shape
    wide, part, span = groups * width, width // FINISH_PARTS, rows // groups
    me = lax.axis_index("grp")
    made = dict(zip(range(2, 17), made))

    def load(i):
        if i < FINISH_PARTS:
            piece = pl.ds(i * part, part)
            return pltpu.make_async_copy(gtok_ref.at[piece], gtok_low.at[piece], in_sem.at[i])
        if i < FINISH_PARTS + 2:
            source, target = ((rest_ref, rest), (qkv_ref, qkv))[i - FINISH_PARTS]
            return pltpu.make_async_copy(source, target, in_sem.at[i])
        j = i - FINISH_PARTS - 2
        columns = ds(xor(me, j, groups) * span, span, span)
        source = result_ref.at[:, columns] if j else own_ref.at[0]
        return pltpu.make_async_copy(source, result.at[:, columns], in_sem.at[i])

    def store(i):
        return pltpu.make_async_copy(made[i], outs[i], out_sem.at[i])

    def store_tokens(i):
        piece = pl.ds(i * part, part)
        return pltpu.make_async_copy(gtok.at[piece], outs[1].at[piece], out_sem.at[17 + i])

    whole = pltpu.make_async_copy(result, outs[0], out_sem.at[0])
    first = FINISH_PARTS + 2
    for i in (*range(first, first + groups), *range(first)):
        load(i).start()
    for j in range(groups):
        load(first + j).wait()
    whole.start()
    for i in range(FINISH_PARTS):
        piece = pl.ds(i * part, part)
        load(i).wait()
        gtok[piece, :] = gtok_low[piece, :].astype(F32)
        store_tokens(i).start()
    load(FINISH_PARTS).wait()
    load(FINISH_PARTS + 1).wait()
    for i in range(3):
        made[2 + i][...] = qkv[:, i * width : (i + 1) * width].astype(F32)
    small = qkv[:, 3 * width : 3 * width + 128].astype(F32).T
    made[5][...] = small[B_QUERY : B_QUERY + 1]
    made[6][...] = small[B_VALUE : B_VALUE + 1]
    made[7][...] = rest[:, 0:wide].astype(F32)
    made[11][...] = rest[:, wide : wide + hidden].astype(F32)
    made[13][...] = rest[:, wide + hidden : wide + 2 * hidden].astype(F32)
    small = rest[:, wide + 2 * hidden : wide + 2 * hidden + 128].astype(F32).T
    for i, which in ((8, B_OUT), (9, GAIN1), (10, SHIFT1), (14, B_BACK), (15, GAIN2), (16, SHIFT2)):
        made[i][...] = small[which : which + 1]
    row = jnp.concatenate(
        [small[B_INTER + a : B_INTER + a + 1] for a in range(hidden // width)], axis=1
    )
    for i in range(hidden // 128):
        made[12][i : i + 1, :] = row[:, i * 128 : (i + 1) * 128]
    for i in range(2, 17):
        store(i).start()
    for i in range(FINISH_PARTS):
        store_tokens(i).wait()
    for i in range(2, 17):
        store(i).wait()
    whole.wait()


def finish(sizes, own, result, grad_tokens, grad_rest, grad_qkv):
    groups, _, _, hidden = sizes
    width, rows = result.shape
    matrix, vector = (width, groups * width), (1, width)
    shapes = [(width, width)] * 3 + [vector] * 2 + [matrix] + [vector] * 3
    shapes += [(width, hidden), (hidden // 128, 128), (width, hidden)] + [vector] * 3
    anywhere = pl.BlockSpec(memory_space=pl.ANY)
    return pl.pallas_call(
        functools.partial(finish_kernel, groups, hidden),
        in_specs=[anywhere] * 5,
        out_specs=[anywhere] * 17,
        out_shape=[jax.ShapeDtypeStruct((width, rows), LOW), jax.ShapeDtypeStruct((width, rows), F32)]
        + [jax.ShapeDtypeStruct(shape, F32) for shape in shapes],
        scratch_shapes=[
            pltpu.VMEM((width, rows), LOW),
            pltpu.VMEM((width, rows), LOW),
            pltpu.VMEM((width, rows), F32),
            pltpu.VMEM(grad_rest.shape, LOW),
            pltpu.VMEM(grad_qkv.shape, LOW),
        ]
        + [pltpu.VMEM(shape, F32) for shape in shapes]
        + [
            pltpu.SemaphoreType.DMA((FINISH_PARTS + 2 + groups,)),
            pltpu.SemaphoreType.DMA((17 + FINISH_PARTS,)),
        ],
        compiler_params=pltpu.CompilerParams(vmem_limit_bytes=VMEM_BYTES),
        name="finish",
    )(own, result, grad_tokens, grad_rest, grad_qkv)


def joined(halves, columns):
    half, whole = round_up(columns, 256) // 2, halves.shape[1]
    if 2 * half == whole:
        return halves
    return jnp.concatenate([halves[:, 0:half], halves[:, whole // 2 : whole // 2 + half]], axis=1)


def local(
    tokens,
    cotangent,
    lengths,
    w_query,
    w_key,
    w_value,
    b_query,
    b_value,
    w_out,
    b_out,
    gain_attn,
    shift_attn,
    w_inter,
    b_inter,
    w_back,
    b_back,
    gain_ffn,
    shift_ffn,
):
    width, rows = tokens.shape
    groups = lax.axis_size("grp")
    plane = Plane(lax.axis_size("seq"), width)
    seq_len = rows // lengths.shape[0]
    hidden = w_inter.shape[1]
    wide = groups * width
    sizes = (groups, plane, seq_len, hidden)

    vectors = [b_query, b_value, b_out, gain_attn, shift_attn, b_back, gain_ffn, shift_ffn, b_inter]
    weights = (w_out, w_inter, w_back, w_query, w_key, w_value)
    vectors = [vector.reshape(1, -1) for vector in vectors[:-1]] + [b_inter.reshape(-1, 128)]
    if plane.size == 8:
        own, _, _, *made = fused(sizes, lengths, tokens, cotangent, weights, vectors)
    else:
        saved = forward(sizes, lengths, tokens, cotangent, weights, vectors)
        own, made = saved[8], backward(sizes, cotangent, saved)
    result, grad_tokens, grad_rest, grad_qkv = made
    grad_rest = joined(grad_rest, wide + 2 * hidden + 128)
    grad_qkv = joined(grad_qkv, 3 * width + 128)
    outs = finish(sizes, own, result, grad_tokens, grad_rest, grad_qkv)
    return tuple(out.reshape(-1) if out.shape[0] < 8 else out for out in outs)


def solution(mesh):
    flat, matrix, vector = P("grp", "seq"), P("grp", None), P("grp")
    return jax.shard_map(
        local,
        mesh=mesh,
        in_specs=(flat, flat, P("seq"), matrix, matrix, matrix, vector, vector, matrix)
        + (vector, vector, vector, matrix, vector, matrix, vector, vector, vector),
        out_specs=(flat, flat, matrix, matrix, matrix, vector, vector, matrix, vector)
        + (vector, vector, matrix, vector, matrix, vector, vector, vector),
        check_vma=False,
    )
```
